512 devices in a mesh: gx: 64 (over x, z, core), vert: 8 (over y).
Axes of the slice: x: 4, y: 8, z: 8, core: 2. Of those that a mesh axis runs over, the one named last changes fastest.
Arguments:
- prior_population: float32 [1024, 8, 32768], P('gx', None, 'vert'), may hold values from 0.1 to 2
- speeds: float32 [3, 32768], P(None, 'vert'), may hold values from 0.05 to 3
- jacobian: float32 [32768], P('vert'), may hold values from 0.5 to 1.5
- octant: int32 [256], P('vert'), may hold values from 0 to 7, as said below
- collision: float32 [1024, 8], P('gx'), may hold values from 1.953125e-05 to 0.6
- solid_mask: int32 [1024, 8], P('gx'), may hold values from 0 to 1, as said below
- wall_state: float32 [32768], P('vert'), may hold values from 0.1 to 2
- inflow: float32 [2, 8, 32768], P(None, None, 'vert'), may hold values from 0.1 to 2
Outputs:
- updated: float32 [1024, 8, 32768], P('gx', None, 'vert')
The draws below stay inside these ranges and needn't reach their ends.
Inputs may be any that keep to these rules, and one draw needn't show every extreme that they name: Among the blocks of each aligned group of 4096 velocities, exactly half have an even octant. `solid_mask`: 1 marks the cells of one disc; the rows from 4 on meet it, the rows before never.
All inputs are finite; a program needn't handle non-finite values.
Results may differ from the reference program's by a relative error of at most 0.0003.
Values sent between devices are 32-bit elements; how exact they have to be, the bound alone decides.
A program may use at most 128 MiB of HBM per device.

```python
import math
import jax
import jax.numpy as jnp
from jax import lax

VEL = 32768
VBLK = 128
ROWS = 8
JAC = 4
V_DEV = 4096
STACK_COUNT = 1024


def octant_values(key):
    key = jax.random.fold_in(key, 11)
    per_group = V_DEV // VBLK
    groups = VEL // V_DEV
    order_keys = jax.random.split(jax.random.fold_in(key, 1), groups)
    ranking = jax.vmap(lambda one_key: jax.random.permutation(one_key, per_group))(order_keys)
    first_bit = (ranking >= per_group // 2).astype(jnp.int32).reshape(-1)
    upper_bits = jax.random.randint(jax.random.fold_in(key, 2), (groups * per_group,), 0, 4)
    return (first_bit + 2 * upper_bits).astype(jnp.int32)


def draw_octant(key, part):
    return octant_values(key)


def draw_prior_population(key, part):
    shared_octant = octant_values(key)
    key = jax.random.fold_in(key, 13)
    octant_all = jnp.repeat(shared_octant, VBLK)
    sign_first = (1 - 2 * (octant_all % 2)).astype(jnp.float32)
    sign_second = (1 - 2 * (octant_all // 2 % 2)).astype(jnp.float32)
    sign_third = (1 - 2 * (octant_all // 4)).astype(jnp.float32)
    tilts = jax.random.uniform(jax.random.fold_in(key, 1), (STACK_COUNT, 3, ROWS), jnp.float32, -1.0 / 6.0, 1.0 / 6.0)
    element_key = jax.random.fold_in(key, 2)
    log_range = math.log(20.0)

    def one_column(column_inputs):
        index, tilt = column_inputs
        element = jax.random.uniform(jax.random.fold_in(element_key, index), (ROWS, VEL), jnp.float32)
        shift = tilt[0][:, None] * sign_first + tilt[1][:, None] * sign_second + tilt[2][:, None] * sign_third
        exponent = 0.4 * element + 0.6 * (0.5 + shift)
        return 0.1 * jnp.exp(exponent * log_range)
    values = lax.map(one_column, (jnp.arange(STACK_COUNT, dtype=jnp.int32), tilts))
    return values.astype(jnp.float32)


def draw_collision(key, part):
    key = jax.random.fold_in(key, 5)
    row_order = jax.random.permutation(jax.random.fold_in(key, 1), ROWS)
    rough_row = row_order < ROWS // 2
    lower = 0.02 / STACK_COUNT
    upper = jnp.where(rough_row, 0.6, 0.5 / STACK_COUNT)[None, :]
    unit = jax.random.uniform(jax.random.fold_in(key, 2), (STACK_COUNT, ROWS), jnp.float32)
    rate = lower * jnp.exp(unit * jnp.log(upper / lower))
    return rate.astype(jnp.float32)


def draw_solid_mask(key, part):
    key = jax.random.fold_in(key, 7)
    key_center = jax.random.fold_in(key, 1)
    key_radius = jax.random.fold_in(key, 2)
    largest = min(8 * ROWS, STACK_COUNT // 4)
    radius = jax.random.randint(key_radius, (), 2 * ROWS, largest + 1)
    center_x = jax.random.randint(key_center, (), STACK_COUNT // 4, 3 * STACK_COUNT // 4)
    center_y = ROWS - ROWS // 2 + radius
    cell_x = jnp.arange(STACK_COUNT, dtype=jnp.int32)[:, None]
    cell_y = jnp.arange(ROWS, dtype=jnp.int32)[None, :]
    inside = (cell_x - center_x) * (cell_x - center_x) + (cell_y - center_y) * (cell_y - center_y) <= radius * radius
    return inside.astype(jnp.int32)


def level_of(stream_key, dims, cuts, smallest, high):
    factor_of = 1.0
    for position, parts in cuts:
        heights = jax.random.uniform(jax.random.fold_in(jax.random.fold_in(stream_key, 6), position), (parts,), jnp.float32, smallest / len(cuts), high / len(cuts))
        factor_of = factor_of * jnp.repeat(jnp.exp(heights), dims[position] // parts).reshape((-1,) + (1,) * (len(dims) - 1 - position))
    return factor_of


def setup_inputs(seed: int = 0) -> dict:
    keys = jax.random.split(jax.random.key(seed), 9)
    prior_population = draw_prior_population(jax.random.fold_in(keys[8], 71), 0)
    speeds = jnp.clip(jnp.exp(math.log(3.0) - 4.0943445 * jax.random.uniform(keys[1], (3, VEL), jnp.float32) ** level_of(keys[1], (3, VEL), ((1, 8),), -0.2, 0.2)), 0.05, 3.0)
    jacobian = jnp.clip(0.5 + 1.0 * jax.random.uniform(keys[2], (VEL,), jnp.float32) ** level_of(keys[2], (VEL,), ((0, 8),), -0.2, 0.2), 0.5, 1.5)
    octant = draw_octant(jax.random.fold_in(keys[8], 71), 0)
    collision = draw_collision(jax.random.fold_in(keys[8], 71), 0)
    solid_mask = draw_solid_mask(jax.random.fold_in(keys[8], 71), 0)
    wall_state = jnp.clip(jnp.exp(math.log(2.0) - 2.9957323 * jax.random.uniform(keys[6], (VEL,), jnp.float32) ** level_of(keys[6], (VEL,), ((0, 8),), -0.2, 0.2)), 0.1, 2.0)
    inflow = jnp.clip(jnp.exp(math.log(2.0) - 2.9957323 * jax.random.uniform(keys[7], (2, ROWS, VEL), jnp.float32) ** level_of(keys[7], (2, ROWS, VEL), ((2, 8),), -0.2, 0.2)), 0.1, 2.0)
    return {"prior_population": prior_population, "speeds": speeds, "jacobian": jacobian, "octant": octant, "collision": collision, "solid_mask": solid_mask, "wall_state": wall_state, "inflow": inflow}


VISCOUS_CONDUCT = 2.0 / 3.0
SOLID_DEPTH = 60.0
LOG_SPAN = 2.0 * math.log(60.0)


def velocity_set(speeds, jacobian, octant):
    octant_all = jnp.repeat(octant, VBLK)
    sign_first = (1 - 2 * (octant_all % 2)).astype(jnp.float32)
    sign_second = (1 - 2 * ((octant_all // 2) % 2)).astype(jnp.float32)
    sign_third = (1 - 2 * (octant_all // 4)).astype(jnp.float32)
    weight = jacobian * speeds[0] * speeds[1] * speeds[2] * (LOG_SPAN ** 3 / VEL)
    return sign_first * speeds[0], sign_second * speeds[1], sign_third * speeds[2], weight


def cell_state(column, velocity):
    velocity_x, velocity_y, velocity_z, weight = velocity
    weighted = column * weight
    particle_concentration = jnp.sum(weighted, -1)
    flow_x = jnp.sum(weighted * velocity_x, -1) / particle_concentration
    flow_y = jnp.sum(weighted * velocity_y, -1) / particle_concentration
    flow_z = jnp.sum(weighted * velocity_z, -1) / particle_concentration
    kinetic_integral = 0.5 * jnp.sum(weighted * (velocity_x * velocity_x + velocity_y * velocity_y + velocity_z * velocity_z), -1)
    bulk_motion_norm = flow_x * flow_x + flow_y * flow_y + flow_z * flow_z
    fluid_warmth = (2.0 * kinetic_integral / particle_concentration - bulk_motion_norm) / 3.0
    peculiar_x_part = velocity_x - flow_x[:, None]
    peculiar_y_part = velocity_y - flow_y[:, None]
    peculiar_z_part = velocity_z - flow_z[:, None]
    peculiar_norm = peculiar_x_part * peculiar_x_part + peculiar_y_part * peculiar_y_part + peculiar_z_part * peculiar_z_part
    conduction_x_part = 0.5 * jnp.sum(weighted * peculiar_x_part * peculiar_norm, -1)
    conduction_y_part = 0.5 * jnp.sum(weighted * peculiar_y_part * peculiar_norm, -1)
    conduction_z_part = 0.5 * jnp.sum(weighted * peculiar_z_part * peculiar_norm, -1)
    gaussian_population = (particle_concentration * (2.0 * math.pi * fluid_warmth) ** -1.5)[:, None] * jnp.exp(-peculiar_norm / (2.0 * fluid_warmth[:, None]))
    skew_correction_multiplier = (peculiar_x_part * conduction_x_part[:, None] + peculiar_y_part * conduction_y_part[:, None] + peculiar_z_part * conduction_z_part[:, None]) * (peculiar_norm / fluid_warmth[:, None] - 5.0)
    relaxed_goal_profile = gaussian_population * (1.0 + (1.0 - VISCOUS_CONDUCT) * skew_correction_multiplier / (5.0 * particle_concentration * fluid_warmth * fluid_warmth)[:, None])
    return particle_concentration, kinetic_integral, bulk_motion_norm, fluid_warmth, peculiar_norm, gaussian_population, relaxed_goal_profile


def reference(prior_population, speeds, jacobian, octant, collision, solid_mask, wall_state, inflow):
    velocity = velocity_set(speeds, jacobian, octant)
    inverse = 1.0 / jnp.abs(velocity[0])

    def advance_cell(incoming, cell_inputs):
        column, rate, walled = cell_inputs
        relaxed_goal_profile = cell_state(column, velocity)[6]
        is_solid = walled == 1
        source = jnp.where(is_solid[:, None], wall_state[None, :], relaxed_goal_profile)
        optical = jnp.where(is_solid, SOLID_DEPTH, rate)
        attenuation = jnp.exp(-optical[:, None] * inverse[None, :])
        outgoing = attenuation * incoming + (1.0 - attenuation) * source
        return outgoing, outgoing

    cell_inputs = (prior_population, collision, solid_mask)
    forward_end, forward_part = lax.scan(advance_cell, inflow[0], cell_inputs)
    backward_end, backward_part = lax.scan(advance_cell, inflow[1], cell_inputs, reverse=True)
    interim_split_portion = jnp.where(velocity[0] > 0, forward_part, backward_part)
    speed_sq = velocity[0] * velocity[0] + velocity[1] * velocity[1] + velocity[2] * velocity[2]
    half_density = jnp.sum(interim_split_portion * velocity[3], -1)
    half_energy = 0.5 * jnp.sum(interim_split_portion * (velocity[3] * speed_sq), -1)

    def site_summary(column):
        state = cell_state(column, velocity)
        return state[0], state[1], state[2], state[3]

    particle_concentration, kinetic_integral, bulk_motion_norm, fluid_warmth = lax.map(site_summary, prior_population)
    iterate_mismatch = jnp.stack([half_density - particle_concentration, half_energy - kinetic_integral])
    row_index = jnp.arange(ROWS)
    nearby_sites = 4.0 - (row_index == 0).astype(jnp.float32) - (row_index == ROWS - 1).astype(jnp.float32)
    denominator_piece = 1.0 + nearby_sites * fluid_warmth
    acceleration_step = iterate_mismatch / denominator_piece
    for counter in range(JAC):
        padded_array = jnp.pad(acceleration_step, ((0, 0), (1, 1), (0, 0)))
        upper_edge_sites = jnp.pad(acceleration_step[:, :, 1:], ((0, 0), (0, 0), (0, 1)))
        lower_edge_sites = jnp.pad(acceleration_step[:, :, :-1], ((0, 0), (0, 0), (1, 0)))
        acceleration_step = (iterate_mismatch + fluid_warmth * (padded_array[:, 2:] + padded_array[:, :-2] + upper_edge_sites + lower_edge_sites)) / denominator_piece
    warmth_increment = (2.0 * acceleration_step[1] / 3.0 - (fluid_warmth + bulk_motion_norm / 3.0) * acceleration_step[0]) / particle_concentration
    mass_ratio = acceleration_step[0] / particle_concentration
    warmth_ratio = warmth_increment / fluid_warmth

    def finished_site(finish_inputs):
        column, half_column, ratio_density, ratio_temp, temp_cell = finish_inputs
        state = cell_state(column, velocity)
        return half_column + state[5] * (ratio_density[:, None] + ratio_temp[:, None] * (state[4] / (2.0 * temp_cell[:, None]) - 1.5))

    return lax.map(finished_site, (prior_population, interim_split_portion, mass_ratio, warmth_ratio, fluid_warmth))
```

```python
import functools
import math

import jax
import jax.numpy as jnp
from jax import lax
from jax.experimental import pallas as pl
from jax.experimental.pallas import tpu as pltpu
from jax.sharding import PartitionSpec as P

VEL = 32768
LANES = 128
JAC = 4
CHUNKS = 4
MOMENTS = 13
SOLID_DEPTH = 60.0
LOG_SPAN = 2.0 * math.log(60.0)
F32 = jnp.float32
MESH = pl.DeviceIdType.MESH

CX, CY, CZ, WEIGHT, WEIGHT_E, NEG_INV, WALL, BACKWARD = range(8)


def lane_block(index):
    return pl.ds(pl.multiple_of(index * LANES, LANES), LANES)


def table_row(base_ref, row, block, rows):
    return jnp.broadcast_to(base_ref[row : row + 1, lane_block(block)], (rows, LANES))


def lane_index(rows):
    return lax.broadcasted_iota(jnp.int32, (rows, LANES), 1)


def moments_kernel(base_ref, prior_ref, out_ref, table, totals):
    columns, rows, width = prior_ref.shape
    blocks = width // LANES
    step = pl.program_id(0)

    @pl.when(step == 0)
    def _():
        totals[...] = jnp.zeros_like(totals)

    for b in range(blocks):
        cx, cy, cz, w = (table_row(base_ref, row, b, rows) for row in (CX, CY, CZ, WEIGHT))
        square = cx * cx + cy * cy + cz * cz
        wx, wy, wz = w * cx, w * cy, w * cz
        entries = (
            w, wx, wy, wz,
            wx * cx, wx * cy, wx * cz, wy * cy, wy * cz, wz * cz,
            wx * square, wy * square, wz * square,
        )
        for m, entry in enumerate(entries):
            table[m, b] = entry

    def pair(g, carry):
        first = [totals[2 * g, m] for m in range(MOMENTS)]
        second = [totals[2 * g + 1, m] for m in range(MOMENTS)]
        for b in range(blocks):
            left = prior_ref[2 * g, :, b * LANES : (b + 1) * LANES]
            right = prior_ref[2 * g + 1, :, b * LANES : (b + 1) * LANES]
            for m in range(MOMENTS):
                entry = table[m, b]
                first[m] = first[m] + left * entry
                second[m] = second[m] + right * entry
        for m in range(MOMENTS):
            totals[2 * g, m] = first[m]
            totals[2 * g + 1, m] = second[m]
        return carry

    lax.fori_loop(0, columns // 2, pair, 0)

    @pl.when(step == pl.num_programs(0) - 1)
    def _():
        lane = lane_index(rows)

        def pack(i, packed):
            packed = list(packed)
            for m in range(MOMENTS):
                total = jnp.sum(totals[i, m], axis=1, keepdims=True)
                spot = lane == (m % 8) * 16 + i
                packed[m // 8] = jnp.where(spot, total, packed[m // 8])
            return tuple(packed)

        zero = jnp.zeros((rows, LANES), F32)
        low, high = lax.fori_loop(0, columns, pack, (zero, zero))
        out_ref[:, :LANES] = low
        out_ref[:, LANES:] = high


def vert_sum_kernel(count, mine_ref, out_ref, slots, send_sem, recv_sem):
    me = lax.axis_index("vert")
    barrier = pltpu.get_barrier_semaphore()
    for k in range(1, count):
        pl.semaphore_signal(
            barrier, inc=1, device_id={"vert": lax.rem(me + k, count)}, device_id_type=MESH
        )
    pl.semaphore_wait(barrier, count - 1)

    def copy_to(k):
        return pltpu.make_async_remote_copy(
            src_ref=mine_ref,
            dst_ref=slots.at[me],
            send_sem=send_sem.at[k],
            recv_sem=recv_sem.at[me],
            device_id={"vert": lax.rem(me + k, count)},
            device_id_type=MESH,
        )

    for k in range(1, count):
        copy_to(k).start()
    slots[me] = mine_ref[...]
    for k in range(1, count):
        other = lax.rem(me + k, count)
        pltpu.make_async_remote_copy(
            src_ref=mine_ref,
            dst_ref=slots.at[other],
            send_sem=send_sem.at[k],
            recv_sem=recv_sem.at[other],
            device_id={"vert": other},
            device_id_type=MESH,
        ).wait_recv()
    total = slots[0]
    for k in range(1, count):
        total = total + slots[k]
    out_ref[...] = total
    for k in range(1, count):
        copy_to(k).wait_send()


def cell_values(sums_ref):
    low, high = sums_ref[:, :LANES], sums_ref[:, LANES:]
    picked = []
    for m in range(MOMENTS):
        source = low if m < 8 else high
        shift = (LANES - 16 * (m % 8)) % LANES
        picked.append(pltpu.roll(source, shift, 1) if shift else source)
    valid = lane_index(low.shape[0]) < 16
    rho = jnp.where(valid, picked[0], 1.0)
    sx, sy, sz, pxx, pxy, pxz, pyy, pyz, pzz, qx, qy, qz = (
        jnp.where(valid, value, 1.0) for value in picked[1:]
    )
    ux, uy, uz = sx / rho, sy / rho, sz / rho
    flow_sq = ux * ux + uy * uy + uz * uz
    second = pxx + pyy + pzz
    warmth = (second / rho - flow_sq) / 3.0
    swirl = rho * flow_sq
    heat_x = 0.5 * (qx - second * ux) - (ux * pxx + uy * pxy + uz * pxz) + swirl * ux
    heat_y = 0.5 * (qy - second * uy) - (ux * pxy + uy * pyy + uz * pyz) + swirl * uy
    heat_z = 0.5 * (qz - second * uz) - (ux * pxz + uy * pyz + uz * pzz) + swirl * uz
    return {
        "rho": rho, "ux": ux, "uy": uy, "uz": uz, "flow_sq": flow_sq, "warmth": warmth,
        "energy": 0.5 * second, "hx": heat_x, "hy": heat_y, "hz": heat_z,
    }


def maxwell_scale(cell):
    warmth = cell["warmth"]
    area = (2.0 * math.pi) * warmth
    return cell["rho"] / (area * jnp.sqrt(area))


def spread(value, column, rows):
    return jnp.broadcast_to(value[:, column : column + 1], (rows, LANES))


def sweep_kernel(octant_ref, sums_ref, base_ref, cell_ref, gain_ref, message_ref, coef):
    columns, rows, width = gain_ref.shape
    blocks = width // LANES
    step = pl.program_id(0)

    @pl.when(step == 0)
    def _():
        cell = cell_values(sums_ref)
        warmth, rho = cell["warmth"], cell["rho"]
        factor = (-2.0 / 3.0) / (5.0 * rho * warmth * warmth)
        values = (
            cell["ux"], cell["uy"], cell["uz"], -0.5 / warmth, maxwell_scale(cell),
            cell["hx"] * factor, cell["hy"] * factor, cell["hz"] * factor,
        )
        for q, value in enumerate(values):
            for i in range(columns):
                coef[q, i] = spread(value, i, rows)

    depth = cell_ref[0, 0]
    for i in range(1, columns):
        depth = depth + cell_ref[0, i]
    diagonal = lane_index(rows) == lax.broadcasted_iota(jnp.int32, (rows, LANES), 0)
    depth_row = jnp.sum(jnp.where(diagonal, depth, 0.0), axis=0, keepdims=True)

    def block(b, carry):
        backward = lax.rem(octant_ref[step * blocks + b], 2)
        cx, cy, cz, neg_inv, wall = (
            table_row(base_ref, row, b, rows) for row in (CX, CY, CZ, NEG_INV, WALL)
        )
        gain = jnp.zeros((rows, LANES), F32)
        for s in range(columns):
            i = s + backward * (columns - 1 - 2 * s)
            px, py, pz = cx - coef[0, i], cy - coef[1, i], cz - coef[2, i]
            exponent = (px * px + py * py + pz * pz) * coef[3, i]
            skew = (px * coef[5, i] + py * coef[6, i] + pz * coef[7, i]) * (exponent + 2.5)
            target = coef[4, i] * jnp.exp(exponent) * (1.0 + skew)
            source = jnp.where(cell_ref[1, i] > 0.5, wall, target)
            attenuation = jnp.exp(cell_ref[0, i] * neg_inv)
            gain = attenuation * gain + (1.0 - attenuation) * source
            gain_ref[i, :, lane_block(b)] = gain
        message_ref[b, 0:rows] = gain
        message_ref[b, rows : rows + 1] = depth_row
        return carry

    lax.fori_loop(0, blocks, block, 0)


def entering_kernel(
    count, message_ref, base_ref, inflow_ref, out_ref,
    arrived, result, incoming, send_sem, recv_sem, back_send_sem, back_recv_sem,
):
    blocks = message_ref.shape[0]
    rows = inflow_ref.shape[1]
    me = lax.axis_index("gx")
    chip = lax.div(me, 2)
    is_owner = lax.rem(me, 2) == 0

    barrier = pltpu.get_barrier_semaphore()

    def greet(k, carry):
        pl.semaphore_signal(
            barrier, inc=1, device_id={"gx": lax.rem(me + k, count)}, device_id_type=MESH
        )
        return carry

    def greet_owner(k, carry):
        pl.semaphore_signal(
            barrier, inc=1, device_id={"gx": 2 * lax.rem(chip + k, blocks)}, device_id_type=MESH
        )
        return carry

    @pl.when(is_owner)
    def _():
        lax.fori_loop(1, count, greet, 0)
        pl.semaphore_wait(barrier, count - 1)

    @pl.when(jnp.logical_not(is_owner))
    def _():
        lax.fori_loop(0, blocks, greet_owner, 0)
        pl.semaphore_wait(barrier, blocks)

    def outgoing(b):
        return pltpu.make_async_remote_copy(
            src_ref=message_ref.at[b],
            dst_ref=arrived.at[me],
            send_sem=send_sem.at[b],
            recv_sem=recv_sem.at[me],
            device_id={"gx": 2 * b},
            device_id_type=MESH,
        )

    def start_out(k, carry):
        b = lax.rem(chip + k, blocks)

        @pl.when(2 * b != me)
        def _():
            outgoing(b).start()

        return carry

    lax.fori_loop(0, blocks, start_out, 0)

    def returning(j):
        return pltpu.make_async_remote_copy(
            src_ref=result.at[j],
            dst_ref=incoming.at[chip],
            send_sem=back_send_sem.at[j],
            recv_sem=back_recv_sem.at[chip],
            device_id={"gx": j},
            device_id_type=MESH,
        )

    @pl.when(is_owner)
    def _():
        arrived[me] = message_ref[chip]

        def wait_in(k, carry):
            j = lax.rem(me + k, count)
            pltpu.make_async_remote_copy(
                src_ref=message_ref.at[chip],
                dst_ref=arrived.at[j],
                send_sem=send_sem.at[chip],
                recv_sem=recv_sem.at[j],
                device_id={"gx": j},
                device_id_type=MESH,
            ).wait_recv()
            return carry

        lax.fori_loop(1, count, wait_in, 0)
        forward = table_row(base_ref, BACKWARD, chip, rows) < 0.5
        neg_inv = table_row(base_ref, NEG_INV, chip, rows)
        diagonal = lane_index(rows) == lax.broadcasted_iota(jnp.int32, (rows, LANES), 0)

        def lap(s, state):
            t = count - 1 - s
            gain = jnp.where(forward, arrived[s, 0:rows], arrived[t, 0:rows])
            depth_row = jnp.where(
                forward[0:1], arrived[s, rows : rows + 1], arrived[t, rows : rows + 1]
            )
            depth_all = jnp.broadcast_to(depth_row, (rows, LANES))
            depth = jnp.sum(jnp.where(diagonal, depth_all, 0.0), axis=1, keepdims=True)
            result[s] = state
            return jnp.exp(depth * neg_inv) * state + gain

        boundary = jnp.where(
            forward, inflow_ref[0, :, lane_block(chip)], inflow_ref[1, :, lane_block(chip)]
        )
        lax.fori_loop(0, count, lap, boundary, unroll=4)

        def flip(s, carry):
            t = count - 1 - s
            low, high = result[s], result[t]
            result[s] = jnp.where(forward, low, high)
            result[t] = jnp.where(forward, high, low)
            return carry

        lax.fori_loop(0, count // 2, flip, 0, unroll=4)

        def start_back(k, carry):
            returning(lax.rem(me + k, count)).start()
            return carry

        lax.fori_loop(1, count, start_back, 0)
        incoming[chip] = result[me]

    def wait_back(b, carry):
        @pl.when(2 * b != me)
        def _():
            pltpu.make_async_remote_copy(
                src_ref=result.at[0],
                dst_ref=incoming.at[b],
                send_sem=back_send_sem.at[0],
                recv_sem=back_recv_sem.at[b],
                device_id={"gx": 2 * b},
                device_id_type=MESH,
            ).wait_recv()

        return carry

    lax.fori_loop(0, blocks, wait_back, 0)
    out_ref[...] = incoming[...]

    def finish_out(b, carry):
        @pl.when(2 * b != me)
        def _():
            outgoing(b).wait_send()

        return carry

    lax.fori_loop(0, blocks, finish_out, 0)

    @pl.when(is_owner)
    def _():
        def finish_back(k, carry):
            returning(lax.rem(me + k, count)).wait_send()
            return carry

        lax.fori_loop(1, count, finish_back, 0)


def running_depth(cell_ref, depth_ref):
    columns = cell_ref.shape[1]
    total = cell_ref[0, 0]
    depth_ref[0, 0] = total
    for i in range(1, columns):
        total = total + cell_ref[0, i]
        depth_ref[0, i] = total
    total = cell_ref[0, columns - 1]
    depth_ref[1, columns - 1] = total
    for i in range(columns - 2, -1, -1):
        total = total + cell_ref[0, i]
        depth_ref[1, i] = total


def half_kernel(octant_ref, sums_ref, base_ref, cell_ref, gain_ref, enter_ref, out_ref, depth, totals):
    columns, rows, width = gain_ref.shape
    blocks = width // LANES
    step = pl.program_id(0)

    @pl.when(step == 0)
    def _():
        running_depth(cell_ref, depth)
        totals[...] = jnp.zeros_like(totals)

    def block(b, sums):
        backward = lax.rem(octant_ref[step * blocks + b], 2)
        neg_inv, weight, weight_e = (
            table_row(base_ref, row, b, rows) for row in (NEG_INV, WEIGHT, WEIGHT_E)
        )
        enter = enter_ref[b]
        sums = list(sums)
        for i in range(columns):
            decay = jnp.exp(depth[backward, i] * neg_inv)
            half = decay * enter + gain_ref[i, :, lane_block(b)]
            sums[i] = sums[i] + half * weight
            sums[columns + i] = sums[columns + i] + half * weight_e
        return tuple(sums)

    sums = tuple(totals[n] for n in range(2 * columns))
    sums = lax.fori_loop(0, blocks, block, sums)
    for n in range(2 * columns):
        totals[n] = sums[n]

    @pl.when(step == pl.num_programs(0) - 1)
    def _():
        cell = cell_values(sums_ref)
        lane = lane_index(rows)
        packed = jnp.zeros((rows, LANES), F32)
        for n, name in ((2, "warmth"), (3, "rho"), (4, "energy")):
            shifted = pltpu.roll(cell[name], 16 * n, 1)
            inside = jnp.logical_and(lane >= 16 * n, lane < 16 * n + 16)
            packed = jnp.where(inside, shifted, packed)
        for n in range(2 * columns):
            total = jnp.sum(sums[n], axis=1, keepdims=True)
            packed = jnp.where(lane == n, total, packed)
        out_ref[...] = packed


def halo_kernel(wide, count, mine_ref, out_ref, slots, send_sem, recv_sem):
    me = lax.axis_index("vert")
    col = lax.axis_index("gx")
    targets = [lax.rem(col + 1, wide), col, lax.rem(col + wide - 1, wide)]
    partners = [(side, k) for side in (0, 1, 2) for k in range(count) if (side, k) != (1, 0)]

    barrier = pltpu.get_barrier_semaphore()
    for side, k in partners:
        pl.semaphore_signal(
            barrier, inc=1,
            device_id={"gx": targets[side], "vert": lax.rem(me + k, count)},
            device_id_type=MESH,
        )
    pl.semaphore_wait(barrier, len(partners))

    def copy_to(side, k):
        return pltpu.make_async_remote_copy(
            src_ref=mine_ref,
            dst_ref=slots.at[side, me],
            send_sem=send_sem.at[side, k],
            recv_sem=recv_sem.at[side, me],
            device_id={"gx": targets[side], "vert": lax.rem(me + k, count)},
            device_id_type=MESH,
        )

    for side, k in partners:
        copy_to(side, k).start()
    slots[1, me] = mine_ref[...]
    for side, k in partners:
        other = lax.rem(me + k, count)
        pltpu.make_async_remote_copy(
            src_ref=mine_ref,
            dst_ref=slots.at[side, other],
            send_sem=send_sem.at[side, k],
            recv_sem=recv_sem.at[side, other],
            device_id={"gx": targets[2 - side], "vert": other},
            device_id_type=MESH,
        ).wait_recv()
    lane = lane_index(mine_ref.shape[0])
    for side in range(3):
        total = slots[side, 0]
        for k in range(1, count):
            total = total + slots[side, k]
        total = jnp.where(lane < 32, total, slots[side, 0])
        if side == 0:
            total = jnp.where(col == 0, 0.0, total)
        if side == 2:
            total = jnp.where(col == wide - 1, 0.0, total)
        out_ref[side] = total
    for side, k in partners:
        copy_to(side, k).wait_send()


def corrections(tiles_ref):
    rows = tiles_ref.shape[1]
    lane = lane_index(rows)
    row = lax.broadcasted_iota(jnp.int32, (rows, LANES), 0)

    def joined(n):
        def moved(side, start, place):
            shift = (place - 16 * n - start) % LANES
            return pltpu.roll(tiles_ref[side], shift, 1) if shift else tiles_ref[side]

        value = jnp.where(lane < 4, moved(0, 12, 0), moved(1, 0, 4))
        value = jnp.where(lane < 20, value, moved(2, 0, 20))
        return jnp.where(lane < 24, value, 0.0)

    warmth = joined(2)
    residuals = [joined(0) - joined(3), joined(1) - joined(4)]
    edges = (row == 0).astype(F32) + (row == rows - 1).astype(F32)
    scale = 1.0 / (1.0 + (4.0 - edges) * warmth)
    out = []
    for residual in residuals:
        value = residual * scale
        for _ in range(JAC):
            around = pltpu.roll(value, 1, 1) + pltpu.roll(value, LANES - 1, 1)
            around = around + jnp.where(row == 0, 0.0, pltpu.roll(value, 1, 0))
            around = around + jnp.where(row == rows - 1, 0.0, pltpu.roll(value, rows - 1, 0))
            value = (residual + warmth * around) * scale
        out.append(pltpu.roll(value, LANES - 4, 1))
    return out


def finish_kernel(
    octant_ref, tiles_ref, sums_ref, base_ref, cell_ref, gain_ref, enter_ref, out_ref, coef, depth
):
    columns, rows, width = gain_ref.shape
    blocks = width // LANES
    step = pl.program_id(0)

    @pl.when(step == 0)
    def _():
        running_depth(cell_ref, depth)
        cell = cell_values(sums_ref)
        rho, warmth = cell["rho"], cell["warmth"]
        change_rho, change_energy = corrections(tiles_ref)
        change_warmth = (
            2.0 * change_energy / 3.0 - (warmth + cell["flow_sq"] / 3.0) * change_rho
        ) / rho
        ratio_rho = change_rho / rho
        ratio_warmth = change_warmth / warmth
        scale = maxwell_scale(cell)
        values = (
            cell["ux"], cell["uy"], cell["uz"], -0.5 / warmth,
            scale * (ratio_rho - 1.5 * ratio_warmth), -(scale * ratio_warmth),
        )
        for q, value in enumerate(values):
            for i in range(columns):
                coef[q, i] = spread(value, i, rows)

    def block(b, carry):
        backward = lax.rem(octant_ref[step * blocks + b], 2)
        cx, cy, cz, neg_inv = (
            table_row(base_ref, row, b, rows) for row in (CX, CY, CZ, NEG_INV)
        )
        enter = enter_ref[b]
        for i in range(columns):
            px, py, pz = cx - coef[0, i], cy - coef[1, i], cz - coef[2, i]
            exponent = (px * px + py * py + pz * pz) * coef[3, i]
            decay = jnp.exp(depth[backward, i] * neg_inv)
            half = decay * enter + gain_ref[i, :, lane_block(b)]
            change = jnp.exp(exponent) * (coef[4, i] + coef[5, i] * exponent)
            out_ref[i, :, lane_block(b)] = half + change
        return carry

    lax.fori_loop(0, blocks, block, 0)


def velocity_table(speeds, jacobian, octant, wall_state):
    def over_lanes(sign):
        return jnp.broadcast_to(sign.astype(F32)[:, None], (octant.shape[0], LANES)).reshape(-1)

    cx = over_lanes(1 - 2 * (octant % 2)) * speeds[0]
    cy = over_lanes(1 - 2 * (octant // 2 % 2)) * speeds[1]
    cz = over_lanes(1 - 2 * (octant // 4)) * speeds[2]
    weight = jacobian * speeds[0] * speeds[1] * speeds[2] * (LOG_SPAN**3 / VEL)
    energy = weight * (0.5 * (cx * cx + cy * cy + cz * cz))
    return jnp.stack(
        [cx, cy, cz, weight, energy, -1.0 / speeds[0], wall_state, over_lanes(octant % 2)]
    )


def per_device(
    wide, count,
    prior_population, speeds, jacobian, octant, collision, solid_mask, wall_state, inflow,
):
    columns, rows, width = prior_population.shape
    blocks = width // LANES
    assert 2 * blocks == wide and columns == 16
    chunk = width // CHUNKS
    part = blocks // CHUNKS
    shape = jax.ShapeDtypeStruct
    whole = pl.BlockSpec(memory_space=pltpu.VMEM)
    scalars = pl.BlockSpec(memory_space=pltpu.SMEM)
    table_spec = pl.BlockSpec((8, chunk), lambda n: (0, n))
    field_spec = pl.BlockSpec((columns, rows, chunk), lambda n: (0, 0, n))
    tile_spec = pl.BlockSpec((part, rows, LANES), lambda n: (n, 0, 0))

    base = velocity_table(speeds, jacobian, octant, wall_state)
    solid = solid_mask == 1
    cell_in = jnp.stack([jnp.where(solid, SOLID_DEPTH, collision), solid.astype(F32)])
    cell_in = jnp.broadcast_to(cell_in[..., None], (2, columns, rows, LANES))

    partial = pl.pallas_call(
        moments_kernel,
        grid=(CHUNKS,),
        out_shape=shape((rows, 2 * LANES), F32),
        in_specs=[table_spec, field_spec],
        out_specs=whole,
        scratch_shapes=[
            pltpu.VMEM((MOMENTS, part, rows, LANES), F32),
            pltpu.VMEM((columns, MOMENTS, rows, LANES), F32),
        ],
    )(base, prior_population)

    sums = pl.pallas_call(
        functools.partial(vert_sum_kernel, count),
        out_shape=shape((rows, 2 * LANES), F32),
        in_specs=[whole],
        out_specs=whole,
        scratch_shapes=[
            pltpu.VMEM((count, rows, 2 * LANES), F32),
            pltpu.SemaphoreType.DMA((count,)),
            pltpu.SemaphoreType.DMA((count,)),
        ],
        compiler_params=pltpu.CompilerParams(collective_id=0, has_side_effects=True),
    )(partial)

    gains, messages = pl.pallas_call(
        sweep_kernel,
        grid=(CHUNKS,),
        out_shape=(shape((columns, rows, width), F32), shape((blocks, rows + 1, LANES), F32)),
        in_specs=[scalars, whole, table_spec, whole],
        out_specs=(field_spec, pl.BlockSpec((part, rows + 1, LANES), lambda n: (n, 0, 0))),
        scratch_shapes=[pltpu.VMEM((8, columns, rows, LANES), F32)],
    )(octant, sums, base, cell_in)

    enter = pl.pallas_call(
        functools.partial(entering_kernel, wide),
        out_shape=shape((blocks, rows, LANES), F32),
        in_specs=[whole, whole, whole],
        out_specs=whole,
        scratch_shapes=[
            pltpu.VMEM((wide, rows + 1, LANES), F32),
            pltpu.VMEM((wide, rows, LANES), F32),
            pltpu.VMEM((blocks, rows, LANES), F32),
            pltpu.SemaphoreType.DMA((blocks,)),
            pltpu.SemaphoreType.DMA((wide,)),
            pltpu.SemaphoreType.DMA((wide,)),
            pltpu.SemaphoreType.DMA((blocks,)),
        ],
        compiler_params=pltpu.CompilerParams(collective_id=1, has_side_effects=True),
    )(messages, base, inflow)

    tile = pl.pallas_call(
        half_kernel,
        grid=(CHUNKS,),
        out_shape=shape((rows, LANES), F32),
        in_specs=[scalars, whole, table_spec, whole, field_spec, tile_spec],
        out_specs=whole,
        scratch_shapes=[
            pltpu.VMEM((2, columns, rows, LANES), F32),
            pltpu.VMEM((2 * columns, rows, LANES), F32),
        ],
    )(octant, sums, base, cell_in, gains, enter)

    tiles = pl.pallas_call(
        functools.partial(halo_kernel, wide, count),
        out_shape=shape((3, rows, LANES), F32),
        in_specs=[whole],
        out_specs=whole,
        scratch_shapes=[
            pltpu.VMEM((3, count, rows, LANES), F32),
            pltpu.SemaphoreType.DMA((3, count)),
            pltpu.SemaphoreType.DMA((3, count)),
        ],
        compiler_params=pltpu.CompilerParams(collective_id=2, has_side_effects=True),
    )(tile)

    return pl.pallas_call(
        finish_kernel,
        grid=(CHUNKS,),
        out_shape=shape((columns, rows, width), F32),
        in_specs=[scalars, whole, whole, table_spec, whole, field_spec, tile_spec],
        out_specs=field_spec,
        scratch_shapes=[
            pltpu.VMEM((6, columns, rows, LANES), F32),
            pltpu.VMEM((2, columns, rows, LANES), F32),
        ],
    )(octant, tiles, sums, base, cell_in, gains, enter)


def solution(mesh):
    in_specs = (
        P("gx", None, "vert"),
        P(None, "vert"),
        P("vert"),
        P("vert"),
        P("gx", None),
        P("gx", None),
        P("vert"),
        P(None, None, "vert"),
    )
    return jax.shard_map(
        functools.partial(per_device, mesh.shape["gx"], mesh.shape["vert"]),
        mesh=mesh,
        in_specs=in_specs,
        out_specs=P("gx", None, "vert"),
        check_vma=False,
    )
```

```python
import functools
import math

import jax
import jax.numpy as jnp
from jax import lax
from jax.experimental import pallas as pl
from jax.experimental.pallas import tpu as pltpu
from jax.sharding import PartitionSpec as P

VEL = 32768
LANES = 128
JAC = 4
CHUNKS = 4
MOMENTS = 13
SOLID_DEPTH = 60.0
LOG_SPAN = 2.0 * math.log(60.0)
F32 = jnp.float32
MESH = pl.DeviceIdType.MESH

CX, CY, CZ, WEIGHT, WEIGHT_E, NEG_INV, WALL = range(7)


def lane_block(index):
    return pl.ds(pl.multiple_of(index * LANES, LANES), LANES)


def lane_index(rows):
    return lax.broadcasted_iota(jnp.int32, (rows, LANES), 1)


def row_index(rows):
    return lax.broadcasted_iota(jnp.int32, (rows, LANES), 0)


def velocity(speeds_ref, octant, block, rows):
    signs = (
        1 - 2 * lax.rem(octant, 2),
        1 - 2 * lax.rem(lax.div(octant, 2), 2),
        1 - 2 * lax.div(octant, 4),
    )
    return [
        jnp.broadcast_to(speeds_ref[n : n + 1, lane_block(block)], (rows, LANES)) * sign.astype(F32)
        for n, sign in enumerate(signs)
    ]


def cell_values(low, high):
    picked = []
    for m in range(MOMENTS):
        source = low if m < 8 else high
        shift = (LANES - 16 * (m % 8)) % LANES
        picked.append(pltpu.roll(source, shift, 1) if shift else source)
    valid = lane_index(low.shape[0]) < 16
    rho, sx, sy, sz, pxx, pxy, pxz, pyy, pyz, pzz, qx, qy, qz = (
        jnp.where(valid, value, 1.0) for value in picked
    )
    ux, uy, uz = sx / rho, sy / rho, sz / rho
    flow_sq = ux * ux + uy * uy + uz * uz
    second = pxx + pyy + pzz
    warmth = (second / rho - flow_sq) / 3.0
    swirl = rho * flow_sq
    heat_x = 0.5 * (qx - second * ux) - (ux * pxx + uy * pxy + uz * pxz) + swirl * ux
    heat_y = 0.5 * (qy - second * uy) - (ux * pxy + uy * pyy + uz * pyz) + swirl * uy
    heat_z = 0.5 * (qz - second * uz) - (ux * pxz + uy * pyz + uz * pzz) + swirl * uz
    return {
        "rho": rho, "ux": ux, "uy": uy, "uz": uz, "flow_sq": flow_sq, "warmth": warmth,
        "energy": 0.5 * second, "hx": heat_x, "hy": heat_y, "hz": heat_z,
    }


def maxwell_scale(cell):
    area = (2.0 * math.pi) * cell["warmth"]
    return cell["rho"] / (area * jnp.sqrt(area))


def spread(value, column, rows):
    return jnp.broadcast_to(value[:, column : column + 1], (rows, LANES))


def fused_kernel(
    wide, count, group_size,
    octant_ref, speeds_ref, jacobian_ref, wall_ref, collision_ref, solid_ref, inflow_ref, prior_ref,
    half_ref, tiles_ref, sums_ref,
    prior, table, moment, cells, att, decay, gain, coef, extra,
    mine, vert_slots, message, arrived, depths, prefix, joint, joint_slots,
    result, incoming, tile, halo_slots,
    prior_sem, vert_send, vert_recv, out_send, out_recv, joint_send, joint_recv,
    back_send, back_recv, halo_send, halo_recv,
):
    columns, rows, width = half_ref.shape
    blocks = width // LANES
    groups = wide // group_size
    me = lax.axis_index("vert")
    col = lax.axis_index("gx")
    group, pos = lax.div(col, group_size), lax.rem(col, group_size)
    diagonal = lane_index(rows) == row_index(rows)
    part = columns // CHUNKS

    def prior_copy(c):
        span = pl.ds(c * part, part)
        return pltpu.make_async_copy(prior_ref.at[span], prior.at[span], prior_sem.at[c])

    for c in range(CHUNKS):
        prior_copy(c).start()

    def in_vert(k):
        return {"vert": lax.rem(me + k, count)}

    def in_group(p):
        return {"gx": group * group_size + p}

    def in_joint(g):
        return {"gx": g * group_size + pos}

    sides = [lax.rem(col + 1, wide), col, lax.rem(col + wide - 1, wide)]
    halo_partners = [(side, k) for side in (0, 1, 2) for k in range(count) if (side, k) != (1, 0)]

    def in_halo(side, k):
        return {"gx": sides[side], "vert": lax.rem(me + k, count)}

    barrier = pltpu.get_barrier_semaphore()

    def greet(device):
        pl.semaphore_signal(barrier, inc=1, device_id=device, device_id_type=MESH)

    for side, k in halo_partners:
        greet(in_halo(side, k))
    for k in range(1, group_size):
        greet(in_group(lax.rem(pos + k, group_size)))
    for k in range(1, groups):
        greet(in_joint(lax.rem(group + k, groups)))

    def build(b, carry):
        cx, cy, cz = velocity(speeds_ref, octant_ref[b], b, rows)
        sx, sy, sz = (
            jnp.broadcast_to(speeds_ref[n : n + 1, lane_block(b)], (rows, LANES)) for n in range(3)
        )
        jac = jnp.broadcast_to(jacobian_ref[:, lane_block(b)], (rows, LANES))
        w = jac * sx * sy * sz * (LOG_SPAN**3 / VEL)
        square = cx * cx + cy * cy + cz * cz
        wx, wy, wz = w * cx, w * cy, w * cz
        table[CX, b] = cx
        table[CY, b] = cy
        table[CZ, b] = cz
        table[WEIGHT, b] = w
        table[WEIGHT_E, b] = w * (0.5 * square)
        table[NEG_INV, b] = -1.0 / sx
        table[WALL, b] = jnp.broadcast_to(wall_ref[:, lane_block(b)], (rows, LANES))
        entries = (
            w, wx, wy, wz,
            wx * cx, wx * cy, wx * cz, wy * cy, wy * cz, wz * cz,
            wx * square, wy * square, wz * square,
        )
        for m, entry in enumerate(entries):
            moment[m, b] = entry
        return carry

    lax.fori_loop(0, blocks, build, 0)

    square_eye = (
        lax.broadcasted_iota(jnp.int32, (rows, rows), 0)
        == lax.broadcasted_iota(jnp.int32, (rows, rows), 1)
    )

    def over_lanes(values):
        stacked = jnp.broadcast_to(values, (rows, rows))
        total = jnp.sum(jnp.where(square_eye, stacked, 0.0), axis=1, keepdims=True)
        return jnp.broadcast_to(total, (rows, LANES))

    total_depth = jnp.zeros((rows, LANES), F32)
    for i in range(columns):
        walled = solid_ref[i : i + 1, :] == 1
        cells[0, i] = over_lanes(jnp.where(walled, SOLID_DEPTH, collision_ref[i : i + 1, :]))
        cells[1, i] = over_lanes(jnp.where(walled, 1.0, 0.0))
        total_depth = total_depth + cells[0, i]
    depth_row = jnp.sum(jnp.where(diagonal, total_depth, 0.0), axis=0, keepdims=True)

    lane = lane_index(rows)

    def pair(g, packed):
        def add(b, sums):
            sums = list(sums)
            left = prior[2 * g, :, lane_block(b)]
            right = prior[2 * g + 1, :, lane_block(b)]
            for m in range(MOMENTS):
                entry = moment[m, b]
                sums[m] = sums[m] + left * entry
                sums[MOMENTS + m] = sums[MOMENTS + m] + right * entry
            return tuple(sums)

        zero = jnp.zeros((rows, LANES), F32)
        sums = lax.fori_loop(0, blocks, add, (zero,) * (2 * MOMENTS), unroll=4)
        packed = list(packed)
        for n in range(2 * MOMENTS):
            m = n % MOMENTS
            total = jnp.sum(sums[n], axis=1, keepdims=True)
            spot = lane == (m % 8) * 16 + 2 * g + n // MOMENTS
            packed[m // 8] = jnp.where(spot, total, packed[m // 8])
        return tuple(packed)

    def moment_chunk(c, packed):
        prior_copy(c).wait()
        return lax.fori_loop(c * (part // 2), (c + 1) * (part // 2), pair, packed)

    zero_tile = jnp.zeros((rows, LANES), F32)
    low, high = lax.fori_loop(0, CHUNKS, moment_chunk, (zero_tile, zero_tile))
    mine[:, :LANES] = low
    mine[:, LANES:] = high

    pl.semaphore_wait(barrier, len(halo_partners) + group_size - 1 + groups - 1)

    def vert_copy(k, slot):
        return pltpu.make_async_remote_copy(
            src_ref=mine, dst_ref=vert_slots.at[slot],
            send_sem=vert_send.at[k], recv_sem=vert_recv.at[slot],
            device_id=in_vert(k), device_id_type=MESH,
        )

    for k in range(1, count):
        vert_copy(k, me).start()

    def decays(b, carry):
        backward = lax.rem(octant_ref[b], 2)
        neg_inv = table[NEG_INV, b]
        running = jnp.ones((rows, LANES), F32)
        for s in range(columns):
            one = jnp.exp(cells[0, s + backward * (columns - 1 - 2 * s)] * neg_inv)
            running = running * one
            att[b, s] = one
            decay[b, s] = running
        return carry

    lax.fori_loop(0, blocks, decays, 0)

    vert_slots[me] = mine[...]
    for k in range(1, count):
        vert_copy(k, lax.rem(me + k, count)).wait_recv()
    total = vert_slots[0]
    for k in range(1, count):
        total = total + vert_slots[k]
    sums_ref[...] = total
    cell = cell_values(total[:, :LANES], total[:, LANES:])
    warmth, rho = cell["warmth"], cell["rho"]
    factor = (-2.0 / 3.0) / (5.0 * rho * warmth * warmth)
    values = (
        cell["ux"], cell["uy"], cell["uz"], -0.5 / warmth, maxwell_scale(cell),
        cell["hx"] * factor, cell["hy"] * factor, cell["hz"] * factor,
    )
    for q, value in enumerate(values):
        for i in range(columns):
            coef[q, i] = spread(value, i, rows)
    packed = zero_tile
    for n, name in ((2, "warmth"), (3, "rho"), (4, "energy")):
        inside = jnp.logical_and(lane >= 16 * n, lane < 16 * n + 16)
        packed = jnp.where(inside, pltpu.roll(cell[name], 16 * n, 1), packed)
    extra[...] = packed

    def out_copy(p, slot):
        return pltpu.make_async_remote_copy(
            src_ref=message.at[p], dst_ref=arrived.at[slot],
            send_sem=out_send.at[p], recv_sem=out_recv.at[slot],
            device_id=in_group(p), device_id_type=MESH,
        )

    def sweep(k, carry):
        p = lax.rem(pos + k, group_size)
        for q in range(2):
            b = 2 * p + q
            backward = lax.rem(octant_ref[b], 2)
            cx, cy, cz, wall = table[CX, b], table[CY, b], table[CZ, b], table[WALL, b]
            running = jnp.zeros((rows, LANES), F32)
            for s in range(columns):
                i = s + backward * (columns - 1 - 2 * s)
                px, py, pz = cx - coef[0, i], cy - coef[1, i], cz - coef[2, i]
                exponent = (px * px + py * py + pz * pz) * coef[3, i]
                skew = (px * coef[5, i] + py * coef[6, i] + pz * coef[7, i]) * (exponent + 2.5)
                target = coef[4, i] * jnp.exp(exponent) * (1.0 + skew)
                source = jnp.where(cells[1, i] > 0.5, wall, target)
                one = att[b, s]
                running = one * running + (1.0 - one) * source
                gain[b, s] = running
            message[p, q * rows : (q + 1) * rows] = running
        message[p, 2 * rows : 2 * rows + 1] = depth_row

        @pl.when(k < group_size)
        def _():
            out_copy(p, pos).start()

        return carry

    lax.fori_loop(1, group_size + 1, sweep, 0)
    arrived[pos] = message[pos]

    def wait_out(k, carry):
        out_copy(pos, lax.rem(pos + k, group_size)).wait_recv()
        return carry

    lax.fori_loop(1, group_size, wait_out, 0)

    for j in range(group_size):
        row = jnp.broadcast_to(arrived[j, 2 * rows : 2 * rows + 1], (rows, LANES))
        depth = jnp.sum(jnp.where(diagonal, row, 0.0), axis=1, keepdims=True)
        depths[j] = jnp.broadcast_to(depth, (rows, LANES))
    backwards = [lax.rem(octant_ref[2 * pos + q], 2) for q in range(2)]
    for q in range(2):
        neg_inv = table[NEG_INV, 2 * pos + q]
        kept, running = jnp.ones((rows, LANES), F32), jnp.zeros((rows, LANES), F32)
        for s in range(group_size):
            t = s + backwards[q] * (group_size - 1 - 2 * s)
            prefix[0, q, s] = kept
            prefix[1, q, s] = running
            one = jnp.exp(depths[t] * neg_inv)
            running = one * running + arrived[t, q * rows : (q + 1) * rows]
            kept = kept * one
        joint[q] = running
        joint[2 + q] = kept

    def joint_copy(g, slot):
        return pltpu.make_async_remote_copy(
            src_ref=joint, dst_ref=joint_slots.at[slot],
            send_sem=joint_send.at[g], recv_sem=joint_recv.at[slot],
            device_id=in_joint(g), device_id_type=MESH,
        )

    for k in range(1, groups):
        joint_copy(lax.rem(group + k, groups), group).start()
    joint_slots[group] = joint[...]
    for k in range(1, groups):
        joint_copy(group, lax.rem(group + k, groups)).wait_recv()
    entering = []
    for q in range(2):
        state = inflow_ref[backwards[q], :, lane_block(2 * pos + q)]
        place = group + backwards[q] * (groups - 1 - 2 * group)
        for s in range(groups - 1):
            g = s + backwards[q] * (groups - 1 - 2 * s)
            before = jnp.broadcast_to((place - s).astype(F32), (rows, LANES)) > 0.5
            longer = joint_slots[g, 2 + q] * state + joint_slots[g, q]
            state = jnp.where(before, longer, state)
        entering.append(state)

    def back_copy(j, slot):
        return pltpu.make_async_remote_copy(
            src_ref=result.at[j], dst_ref=incoming.at[slot],
            send_sem=back_send.at[j], recv_sem=back_recv.at[slot],
            device_id=in_group(j), device_id_type=MESH,
        )

    def send_back(k, carry):
        j = lax.rem(pos + k, group_size)
        for q in range(2):
            s = j + backwards[q] * (group_size - 1 - 2 * j)
            result[j, q] = prefix[0, q, s] * carry[q] + prefix[1, q, s]

        @pl.when(k < group_size)
        def _():
            back_copy(j, pos).start()

        return carry

    lax.fori_loop(1, group_size + 1, send_back, tuple(entering))
    incoming[pos] = result[pos]

    def halves(k, sums):
        p = lax.rem(pos + group_size - k, group_size)

        @pl.when(k > 0)
        def _():
            back_copy(pos, p).wait_recv()

        sums = list(sums)
        for q in range(2):
            b = 2 * p + q
            backward = lax.rem(octant_ref[b], 2)
            weight, weight_e = table[WEIGHT, b], table[WEIGHT_E, b]
            enter = incoming[p, q]
            for i in range(columns):
                s = i + backward * (columns - 1 - 2 * i)
                half = decay[b, s] * enter + gain[b, s]
                half_ref[i, :, lane_block(b)] = half
                sums[i] = sums[i] + half * weight
                sums[columns + i] = sums[columns + i] + half * weight_e
        return tuple(sums)

    sums = lax.fori_loop(0, group_size, halves, (zero_tile,) * (2 * columns))
    packed = extra[...]
    for n in range(2 * columns):
        packed = jnp.where(lane == n, jnp.sum(sums[n], axis=1, keepdims=True), packed)
    tile[...] = packed

    def halo_copy(side, k, slot):
        return pltpu.make_async_remote_copy(
            src_ref=tile, dst_ref=halo_slots.at[side, slot],
            send_sem=halo_send.at[side, k], recv_sem=halo_recv.at[side, slot],
            device_id=in_halo(side, k), device_id_type=MESH,
        )

    for side, k in halo_partners:
        halo_copy(side, k, me).start()
    halo_slots[1, me] = tile[...]
    for side, k in halo_partners:
        halo_copy(side, k, lax.rem(me + k, count)).wait_recv()
    for side in range(3):
        total = halo_slots[side, 0]
        for k in range(1, count):
            total = total + halo_slots[side, k]
        total = jnp.where(lane < 2 * columns, total, halo_slots[side, 0])
        if side == 0:
            total = jnp.where(col == 0, 0.0, total)
        if side == 2:
            total = jnp.where(col == wide - 1, 0.0, total)
        tiles_ref[side] = total

    for k in range(1, count):
        vert_copy(k, me).wait_send()
    for k in range(1, groups):
        joint_copy(lax.rem(group + k, groups), group).wait_send()

    def finish_sends(k, carry):
        p = lax.rem(pos + k, group_size)
        out_copy(p, pos).wait_send()
        back_copy(p, pos).wait_send()
        return carry

    lax.fori_loop(1, group_size, finish_sends, 0)
    for side, k in halo_partners:
        halo_copy(side, k, me).wait_send()


def corrections(tiles_ref):
    rows = tiles_ref.shape[1]
    lane, row = lane_index(rows), row_index(rows)

    def joined(n):
        def moved(side, start, place):
            shift = (place - 16 * n - start) % LANES
            return pltpu.roll(tiles_ref[side], shift, 1) if shift else tiles_ref[side]

        value = jnp.where(lane < 4, moved(0, 12, 0), moved(1, 0, 4))
        value = jnp.where(lane < 20, value, moved(2, 0, 20))
        return jnp.where(lane < 24, value, 0.0)

    warmth = joined(2)
    residuals = [joined(0) - joined(3), joined(1) - joined(4)]
    edges = (row == 0).astype(F32) + (row == rows - 1).astype(F32)
    scale = 1.0 / (1.0 + (4.0 - edges) * warmth)
    out = []
    for residual in residuals:
        value = residual * scale
        for _ in range(JAC):
            around = pltpu.roll(value, 1, 1) + pltpu.roll(value, LANES - 1, 1)
            around = around + jnp.where(row == 0, 0.0, pltpu.roll(value, 1, 0))
            around = around + jnp.where(row == rows - 1, 0.0, pltpu.roll(value, rows - 1, 0))
            value = (residual + warmth * around) * scale
        out.append(pltpu.roll(value, LANES - 4, 1))
    return out


def finish_kernel(octant_ref, tiles_ref, sums_ref, speeds_ref, half_ref, out_ref, coef):
    columns, rows, width = half_ref.shape
    blocks = width // LANES
    step = pl.program_id(0)

    @pl.when(step == 0)
    def _():
        cell = cell_values(sums_ref[:, :LANES], sums_ref[:, LANES:])
        rho, warmth = cell["rho"], cell["warmth"]
        change_rho, change_energy = corrections(tiles_ref)
        change_warmth = (
            2.0 * change_energy / 3.0 - (warmth + cell["flow_sq"] / 3.0) * change_rho
        ) / rho
        ratio_rho = change_rho / rho
        ratio_warmth = change_warmth / warmth
        scale = maxwell_scale(cell)
        values = (
            cell["ux"], cell["uy"], cell["uz"], -0.5 / warmth,
            scale * (ratio_rho - 1.5 * ratio_warmth), -(scale * ratio_warmth),
        )
        for q, value in enumerate(values):
            for i in range(columns):
                coef[q, i] = spread(value, i, rows)

    def block(b, carry):
        cx, cy, cz = velocity(speeds_ref, octant_ref[step * blocks + b], b, rows)
        for i in range(columns):
            px, py, pz = cx - coef[0, i], cy - coef[1, i], cz - coef[2, i]
            exponent = (px * px + py * py + pz * pz) * coef[3, i]
            change = jnp.exp(exponent) * (coef[4, i] + coef[5, i] * exponent)
            out_ref[i, :, lane_block(b)] = half_ref[i, :, lane_block(b)] + change
        return carry

    lax.fori_loop(0, blocks, block, 0)


def per_device(
    wide, count,
    prior_population, speeds, jacobian, octant, collision, solid_mask, wall_state, inflow,
):
    columns, rows, width = prior_population.shape
    blocks = width // LANES
    group_size = blocks // 2
    groups = wide // group_size
    assert groups * group_size == wide and columns == 16
    chunk = width // CHUNKS
    shape = jax.ShapeDtypeStruct
    whole = pl.BlockSpec(memory_space=pltpu.VMEM)
    scalars = pl.BlockSpec(memory_space=pltpu.SMEM)
    field_spec = pl.BlockSpec((columns, rows, chunk), lambda n: (0, 0, n))

    def tiles(*lead):
        return pltpu.VMEM(lead + (rows, LANES), F32)

    half, halo_tiles, sums = pl.pallas_call(
        functools.partial(fused_kernel, wide, count, group_size),
        out_shape=(
            shape((columns, rows, width), F32),
            shape((3, rows, LANES), F32),
            shape((rows, 2 * LANES), F32),
        ),
        in_specs=[scalars] + [whole] * 6 + [pl.BlockSpec(memory_space=pl.ANY)],
        out_specs=(whole, whole, whole),
        scratch_shapes=[
            pltpu.VMEM((columns, rows, width), F32),
            tiles(7, blocks),
            tiles(MOMENTS, blocks),
            tiles(2, columns),
            tiles(blocks, columns),
            tiles(blocks, columns),
            tiles(blocks, columns),
            tiles(8, columns),
            tiles(),
            pltpu.VMEM((rows, 2 * LANES), F32),
            pltpu.VMEM((count, rows, 2 * LANES), F32),
            pltpu.VMEM((group_size, 2 * rows + 1, LANES), F32),
            pltpu.VMEM((group_size, 2 * rows + 1, LANES), F32),
            tiles(group_size),
            tiles(2, 2, group_size),
            tiles(4),
            tiles(groups, 4),
            tiles(group_size, 2),
            tiles(group_size, 2),
            tiles(),
            tiles(3, count),
            pltpu.SemaphoreType.DMA((CHUNKS,)),
            pltpu.SemaphoreType.DMA((count,)),
            pltpu.SemaphoreType.DMA((count,)),
            pltpu.SemaphoreType.DMA((group_size,)),
            pltpu.SemaphoreType.DMA((group_size,)),
            pltpu.SemaphoreType.DMA((groups,)),
            pltpu.SemaphoreType.DMA((groups,)),
            pltpu.SemaphoreType.DMA((group_size,)),
            pltpu.SemaphoreType.DMA((group_size,)),
            pltpu.SemaphoreType.DMA((3, count)),
            pltpu.SemaphoreType.DMA((3, count)),
        ],
        compiler_params=pltpu.CompilerParams(
            collective_id=0, has_side_effects=True, vmem_limit_bytes=40 * 1024 * 1024
        ),
    )(
        octant, speeds, jacobian.reshape(1, width), wall_state.reshape(1, width),
        collision, solid_mask, inflow, prior_population,
    )

    return pl.pallas_call(
        finish_kernel,
        grid=(CHUNKS,),
        out_shape=shape((columns, rows, width), F32),
        in_specs=[
            scalars, whole, whole, pl.BlockSpec((3, chunk), lambda n: (0, n)), field_spec,
        ],
        out_specs=field_spec,
        scratch_shapes=[tiles(6, columns)],
    )(octant, halo_tiles, sums, speeds, half)


def solution(mesh):
    in_specs = (
        P("gx", None, "vert"),
        P(None, "vert"),
        P("vert"),
        P("vert"),
        P("gx", None),
        P("gx", None),
        P("vert"),
        P(None, None, "vert"),
    )
    return jax.shard_map(
        functools.partial(per_device, mesh.shape["gx"], mesh.shape["vert"]),
        mesh=mesh,
        in_specs=in_specs,
        out_specs=P("gx", None, "vert"),
        check_vma=False,
    )
```

```python
import functools
import math

import jax
import jax.numpy as jnp
from jax import lax
from jax.experimental import pallas as pl
from jax.experimental.pallas import tpu as pltpu
from jax.sharding import PartitionSpec as P

VEL = 32768
LANES = 128
JAC = 4
CHUNKS = 4
MOMENTS = 13
SOLID_DEPTH = 60.0
LOG_SPAN = 2.0 * math.log(60.0)
F32 = jnp.float32
MESH = pl.DeviceIdType.MESH

CX, CY, CZ, WEIGHT, WEIGHT_E, NEG_INV, WALL = range(7)


def lane_block(index):
    return pl.ds(pl.multiple_of(index * LANES, LANES), LANES)


def lane_index(rows):
    return lax.broadcasted_iota(jnp.int32, (rows, LANES), 1)


def row_index(rows):
    return lax.broadcasted_iota(jnp.int32, (rows, LANES), 0)


def velocity(speeds_ref, octant, block, rows):
    signs = (
        1 - 2 * lax.rem(octant, 2),
        1 - 2 * lax.rem(lax.div(octant, 2), 2),
        1 - 2 * lax.div(octant, 4),
    )
    return [
        jnp.broadcast_to(speeds_ref[n : n + 1, lane_block(block)], (rows, LANES)) * sign.astype(F32)
        for n, sign in enumerate(signs)
    ]


def cell_values(low, high):
    picked = []
    for m in range(MOMENTS):
        source = low if m < 8 else high
        shift = (LANES - 16 * (m % 8)) % LANES
        picked.append(pltpu.roll(source, shift, 1) if shift else source)
    valid = lane_index(low.shape[0]) < 16
    rho, sx, sy, sz, pxx, pxy, pxz, pyy, pyz, pzz, qx, qy, qz = (
        jnp.where(valid, value, 1.0) for value in picked
    )
    ux, uy, uz = sx / rho, sy / rho, sz / rho
    flow_sq = ux * ux + uy * uy + uz * uz
    second = pxx + pyy + pzz
    warmth = (second / rho - flow_sq) / 3.0
    swirl = rho * flow_sq
    heat_x = 0.5 * (qx - second * ux) - (ux * pxx + uy * pxy + uz * pxz) + swirl * ux
    heat_y = 0.5 * (qy - second * uy) - (ux * pxy + uy * pyy + uz * pyz) + swirl * uy
    heat_z = 0.5 * (qz - second * uz) - (ux * pxz + uy * pyz + uz * pzz) + swirl * uz
    return {
        "rho": rho, "ux": ux, "uy": uy, "uz": uz, "flow_sq": flow_sq, "warmth": warmth,
        "energy": 0.5 * second, "hx": heat_x, "hy": heat_y, "hz": heat_z,
    }


def maxwell_scale(cell):
    area = (2.0 * math.pi) * cell["warmth"]
    return cell["rho"] / (area * jnp.sqrt(area))


def spread(value, column, rows):
    return jnp.broadcast_to(value[:, column : column + 1], (rows, LANES))


def fused_kernel(
    wide, count, group_size,
    octant_in, speeds_in, jacobian_in, wall_in, collision_in, solid_in, inflow_in, prior_in,
    out_ref,
    octant_ref, speeds_ref, jacobian_ref, wall_ref, collision_ref, solid_ref, inflow_ref, prior,
    table, moment, totals, cells, att, decay, gain, power, bell, coef, extra, tiles_ref,
    mine, vert_slots, message, arrived, depths, prefix, joint, joint_slots,
    result, incoming, tile, halo_slots,
    argument_sem, prior_sem, vert_send, vert_recv, out_send, out_recv, joint_send, joint_recv,
    back_send, back_recv, halo_send, halo_recv,
):
    columns, rows, width = out_ref.shape
    blocks = width // LANES
    groups = wide // group_size
    me = lax.axis_index("vert")
    col = lax.axis_index("gx")
    group, pos = lax.div(col, group_size), lax.rem(col, group_size)
    diagonal = lane_index(rows) == row_index(rows)
    part = columns // CHUNKS

    def prior_copy(c):
        span = pl.ds(c * part, part)
        return pltpu.make_async_copy(prior_in.at[span], prior.at[span], prior_sem.at[c])

    owned = pl.ds(pl.multiple_of(pos * (2 * LANES), 2 * LANES), 2 * LANES)
    pairs = (
        (octant_in, octant_ref), (speeds_in, speeds_ref), (jacobian_in, jacobian_ref),
        (wall_in, wall_ref), (collision_in, collision_ref), (solid_in, solid_ref),
        (inflow_in.at[:, :, owned], inflow_ref),
    )
    arguments = [
        pltpu.make_async_copy(source, target, argument_sem.at[n])
        for n, (source, target) in enumerate(pairs)
    ]
    for copy in arguments[:3]:
        copy.start()
    for c in range(CHUNKS):
        prior_copy(c).start()
    for copy in arguments[3:]:
        copy.start()

    def in_vert(k):
        return {"vert": lax.rem(me + k, count)}

    def in_group(p):
        return {"gx": group * group_size + p}

    def in_joint(g):
        return {"gx": g * group_size + pos}

    sides = [lax.rem(col + 1, wide), col, lax.rem(col + wide - 1, wide)]
    halo_partners = [(side, k) for side in (0, 1, 2) for k in range(count) if (side, k) != (1, 0)]

    def in_halo(side, k):
        return {"gx": sides[side], "vert": lax.rem(me + k, count)}

    barrier = pltpu.get_barrier_semaphore()

    def greet(device):
        pl.semaphore_signal(barrier, inc=1, device_id=device, device_id_type=MESH)

    for side, k in halo_partners:
        greet(in_halo(side, k))
    for k in range(1, group_size):
        greet(in_group(lax.rem(pos + k, group_size)))
    for k in range(1, groups):
        greet(in_joint(lax.rem(group + k, groups)))

    for copy in arguments[:3]:
        copy.wait()

    def build(b, carry):
        cx, cy, cz = velocity(speeds_ref, octant_ref[b], b, rows)
        sx, sy, sz = (
            jnp.broadcast_to(speeds_ref[n : n + 1, lane_block(b)], (rows, LANES)) for n in range(3)
        )
        jac = jnp.broadcast_to(jacobian_ref[:, lane_block(b)], (rows, LANES))
        w = jac * sx * sy * sz * (LOG_SPAN**3 / VEL)
        square = cx * cx + cy * cy + cz * cz
        wx, wy, wz = w * cx, w * cy, w * cz
        table[CX, b] = cx
        table[CY, b] = cy
        table[CZ, b] = cz
        table[WEIGHT, b] = w
        table[WEIGHT_E, b] = w * (0.5 * square)
        entries = (
            w, wx, wy, wz,
            wx * cx, wx * cy, wx * cz, wy * cy, wy * cz, wz * cz,
            wx * square, wy * square, wz * square,
        )
        for m, entry in enumerate(entries):
            moment[m, b] = entry
        return carry

    lax.fori_loop(0, blocks, build, 0)

    lane = lane_index(rows)

    zero_tile = jnp.zeros((rows, LANES), F32)

    def pair(g, carry):
        def add(b, sums):
            sums = list(sums)
            left = prior[2 * g, :, lane_block(b)]
            right = prior[2 * g + 1, :, lane_block(b)]
            for m in range(MOMENTS):
                entry = moment[m, b]
                sums[m] = sums[m] + left * entry
                sums[MOMENTS + m] = sums[MOMENTS + m] + right * entry
            return tuple(sums)

        sums = lax.fori_loop(0, blocks, add, (zero_tile,) * (2 * MOMENTS), unroll=4)
        for m in range(MOMENTS):
            totals[2 * g, m] = sums[m]
            totals[2 * g + 1, m] = sums[MOMENTS + m]
        return carry

    def moment_chunk(c, carry):
        prior_copy(c).wait()
        return lax.fori_loop(c * (part // 2), (c + 1) * (part // 2), pair, carry)

    lax.fori_loop(0, CHUNKS, moment_chunk, 0)

    def pack(c, packed):
        packed = list(packed)
        for n in range(part):
            for m in range(MOMENTS):
                total = jnp.sum(totals[c * part + n, m], axis=1, keepdims=True)
                spot = lane == (m % 8) * 16 + c * part + n
                packed[m // 8] = jnp.where(spot, total, packed[m // 8])
        return tuple(packed)

    low, high = lax.fori_loop(0, CHUNKS, pack, (zero_tile, zero_tile))
    mine[:, :LANES] = low
    mine[:, LANES:] = high

    pl.semaphore_wait(barrier, len(halo_partners) + group_size - 1 + groups - 1)

    def vert_copy(k, slot):
        return pltpu.make_async_remote_copy(
            src_ref=mine, dst_ref=vert_slots.at[slot],
            send_sem=vert_send.at[k], recv_sem=vert_recv.at[slot],
            device_id=in_vert(k), device_id_type=MESH,
        )

    for k in range(1, count):
        vert_copy(k, me).start()

    for copy in arguments[3:]:
        copy.wait()
    walled = solid_ref[...] == 1
    optical = jnp.where(walled, SOLID_DEPTH, collision_ref[...])
    flags = jnp.where(walled, 1.0, 0.0)
    total_depth = zero_tile
    for i in range(columns):
        cells[0, i] = spread(optical, i, rows)
        cells[1, i] = spread(flags, i, rows)
        total_depth = total_depth + cells[0, i]
    depth_row = jnp.sum(jnp.where(diagonal, total_depth, 0.0), axis=0, keepdims=True)

    def decays(b, carry):
        backward = lax.rem(octant_ref[b], 2)
        speed = jnp.broadcast_to(speeds_ref[0:1, lane_block(b)], (rows, LANES))
        neg_inv = -1.0 / speed
        table[NEG_INV, b] = neg_inv
        table[WALL, b] = jnp.broadcast_to(wall_ref[:, lane_block(b)], (rows, LANES))
        running = jnp.ones((rows, LANES), F32)
        for s in range(columns):
            one = jnp.exp(cells[0, s + backward * (columns - 1 - 2 * s)] * neg_inv)
            running = running * one
            att[b, s] = one
            decay[b, s] = running
        return carry

    lax.fori_loop(0, blocks, decays, 0)

    vert_slots[me] = mine[...]
    for k in range(1, count):
        vert_copy(k, lax.rem(me + k, count)).wait_recv()
    total = vert_slots[0]
    for k in range(1, count):
        total = total + vert_slots[k]
    cell = cell_values(total[:, :LANES], total[:, LANES:])
    warmth, rho = cell["warmth"], cell["rho"]
    scale = maxwell_scale(cell)
    factor = (-2.0 / 3.0) / (5.0 * rho * warmth * warmth)
    values = (
        cell["ux"], cell["uy"], cell["uz"], -0.5 / warmth, scale,
        cell["hx"] * factor, cell["hy"] * factor, cell["hz"] * factor,
    )
    for q, value in enumerate(values):
        for i in range(columns):
            coef[q, i] = spread(value, i, rows)
    packed = zero_tile
    for n, name in ((2, "warmth"), (3, "rho"), (4, "energy")):
        inside = jnp.logical_and(lane >= 16 * n, lane < 16 * n + 16)
        packed = jnp.where(inside, pltpu.roll(cell[name], 16 * n, 1), packed)
    extra[0] = packed
    for n, value in enumerate((rho, warmth, cell["flow_sq"], scale)):
        extra[1 + n] = value

    def out_copy(p, slot):
        return pltpu.make_async_remote_copy(
            src_ref=message.at[p], dst_ref=arrived.at[slot],
            send_sem=out_send.at[p], recv_sem=out_recv.at[slot],
            device_id=in_group(p), device_id_type=MESH,
        )

    def sweep(k, carry):
        p = lax.rem(pos + k, group_size)
        for q in range(2):
            b = 2 * p + q
            backward = lax.rem(octant_ref[b], 2)
            cx, cy, cz, wall = table[CX, b], table[CY, b], table[CZ, b], table[WALL, b]
            running = jnp.zeros((rows, LANES), F32)
            for s in range(columns):
                i = s + backward * (columns - 1 - 2 * s)
                px, py, pz = cx - coef[0, i], cy - coef[1, i], cz - coef[2, i]
                exponent = (px * px + py * py + pz * pz) * coef[3, i]
                skew = (px * coef[5, i] + py * coef[6, i] + pz * coef[7, i]) * (exponent + 2.5)
                weight = jnp.exp(exponent)
                power[b, s] = exponent
                bell[b, s] = weight
                target = coef[4, i] * weight * (1.0 + skew)
                source = jnp.where(cells[1, i] > 0.5, wall, target)
                one = att[b, s]
                running = one * running + (1.0 - one) * source
                gain[b, s] = running
            message[p, q * rows : (q + 1) * rows] = running
        message[p, 2 * rows : 2 * rows + 1] = depth_row

        @pl.when(k < group_size)
        def _():
            out_copy(p, pos).start()

        return carry

    lax.fori_loop(1, group_size + 1, sweep, 0)
    arrived[pos] = message[pos]

    def wait_out(k, carry):
        out_copy(pos, lax.rem(pos + k, group_size)).wait_recv()
        return carry

    lax.fori_loop(1, group_size, wait_out, 0)

    for j in range(group_size):
        row = jnp.broadcast_to(arrived[j, 2 * rows : 2 * rows + 1], (rows, LANES))
        depth = jnp.sum(jnp.where(diagonal, row, 0.0), axis=1, keepdims=True)
        depths[j] = jnp.broadcast_to(depth, (rows, LANES))
    backwards = [lax.rem(octant_ref[2 * pos + q], 2) for q in range(2)]
    for q in range(2):
        neg_inv = table[NEG_INV, 2 * pos + q]
        kept, running = jnp.ones((rows, LANES), F32), jnp.zeros((rows, LANES), F32)
        for s in range(group_size):
            t = s + backwards[q] * (group_size - 1 - 2 * s)
            prefix[0, q, s] = kept
            prefix[1, q, s] = running
            one = jnp.exp(depths[t] * neg_inv)
            running = one * running + arrived[t, q * rows : (q + 1) * rows]
            kept = kept * one
        joint[q] = running
        joint[2 + q] = kept

    def joint_copy(g, slot):
        return pltpu.make_async_remote_copy(
            src_ref=joint, dst_ref=joint_slots.at[slot],
            send_sem=joint_send.at[g], recv_sem=joint_recv.at[slot],
            device_id=in_joint(g), device_id_type=MESH,
        )

    for k in range(1, groups):
        joint_copy(lax.rem(group + k, groups), group).start()
    joint_slots[group] = joint[...]
    for k in range(1, groups):
        joint_copy(group, lax.rem(group + k, groups)).wait_recv()
    entering = []
    for q in range(2):
        state = inflow_ref[backwards[q], :, q * LANES : (q + 1) * LANES]
        place = group + backwards[q] * (groups - 1 - 2 * group)
        for s in range(groups - 1):
            g = s + backwards[q] * (groups - 1 - 2 * s)
            before = jnp.broadcast_to((place - s).astype(F32), (rows, LANES)) > 0.5
            longer = joint_slots[g, 2 + q] * state + joint_slots[g, q]
            state = jnp.where(before, longer, state)
        entering.append(state)

    def back_copy(j, slot):
        return pltpu.make_async_remote_copy(
            src_ref=result.at[j], dst_ref=incoming.at[slot],
            send_sem=back_send.at[j], recv_sem=back_recv.at[slot],
            device_id=in_group(j), device_id_type=MESH,
        )

    def send_back(k, carry):
        j = lax.rem(pos + k, group_size)
        for q in range(2):
            s = j + backwards[q] * (group_size - 1 - 2 * j)
            result[j, q] = prefix[0, q, s] * carry[q] + prefix[1, q, s]

        @pl.when(k < group_size)
        def _():
            back_copy(j, pos).start()

        return carry

    lax.fori_loop(1, group_size + 1, send_back, tuple(entering))
    incoming[pos] = result[pos]

    def halves(k, sums):
        p = lax.rem(pos + group_size - k, group_size)

        @pl.when(k > 0)
        def _():
            back_copy(pos, p).wait_recv()

        sums = list(sums)
        for q in range(2):
            b = 2 * p + q
            backward = lax.rem(octant_ref[b], 2)
            weight, weight_e = table[WEIGHT, b], table[WEIGHT_E, b]
            enter = incoming[p, q]
            for i in range(columns):
                s = i + backward * (columns - 1 - 2 * i)
                half = decay[b, s] * enter + gain[b, s]
                out_ref[i, :, lane_block(b)] = half
                sums[i] = sums[i] + half * weight
                sums[columns + i] = sums[columns + i] + half * weight_e
        return tuple(sums)

    sums = lax.fori_loop(0, group_size, halves, (zero_tile,) * (2 * columns))
    packed = extra[0]
    for n in range(2 * columns):
        packed = jnp.where(lane == n, jnp.sum(sums[n], axis=1, keepdims=True), packed)
    tile[...] = packed

    def halo_copy(side, k, slot):
        return pltpu.make_async_remote_copy(
            src_ref=tile, dst_ref=halo_slots.at[side, slot],
            send_sem=halo_send.at[side, k], recv_sem=halo_recv.at[side, slot],
            device_id=in_halo(side, k), device_id_type=MESH,
        )

    for side, k in halo_partners:
        halo_copy(side, k, me).start()
    halo_slots[1, me] = tile[...]
    for side, k in halo_partners:
        halo_copy(side, k, lax.rem(me + k, count)).wait_recv()
    for side in range(3):
        total = halo_slots[side, 0]
        for k in range(1, count):
            total = total + halo_slots[side, k]
        total = jnp.where(lane < 2 * columns, total, halo_slots[side, 0])
        if side == 0:
            total = jnp.where(col == 0, 0.0, total)
        if side == 2:
            total = jnp.where(col == wide - 1, 0.0, total)
        tiles_ref[side] = total

    rho, warmth, flow_sq, scale = (extra[1 + n] for n in range(4))
    change_rho, change_energy = corrections(tiles_ref)
    change_warmth = (2.0 * change_energy / 3.0 - (warmth + flow_sq / 3.0) * change_rho) / rho
    ratio_rho = change_rho / rho
    ratio_warmth = change_warmth / warmth
    for q, value in enumerate((scale * (ratio_rho - 1.5 * ratio_warmth), -(scale * ratio_warmth))):
        for i in range(columns):
            coef[q, i] = spread(value, i, rows)

    def finish(b, carry):
        backward = lax.rem(octant_ref[b], 2)
        for i in range(columns):
            s = i + backward * (columns - 1 - 2 * i)
            change = bell[b, s] * (coef[0, i] + coef[1, i] * power[b, s])
            out_ref[i, :, lane_block(b)] = out_ref[i, :, lane_block(b)] + change
        return carry

    lax.fori_loop(0, blocks, finish, 0)

    for k in range(1, count):
        vert_copy(k, me).wait_send()
    for k in range(1, groups):
        joint_copy(lax.rem(group + k, groups), group).wait_send()

    def finish_sends(k, carry):
        p = lax.rem(pos + k, group_size)
        out_copy(p, pos).wait_send()
        back_copy(p, pos).wait_send()
        return carry

    lax.fori_loop(1, group_size, finish_sends, 0)
    for side, k in halo_partners:
        halo_copy(side, k, me).wait_send()


def corrections(tiles_ref):
    rows = tiles_ref.shape[1]
    lane, row = lane_index(rows), row_index(rows)

    def joined(n):
        def moved(side, start, place):
            shift = (place - 16 * n - start) % LANES
            return pltpu.roll(tiles_ref[side], shift, 1) if shift else tiles_ref[side]

        value = jnp.where(lane < 4, moved(0, 12, 0), moved(1, 0, 4))
        value = jnp.where(lane < 20, value, moved(2, 0, 20))
        return jnp.where(lane < 24, value, 0.0)

    warmth = joined(2)
    residuals = [joined(0) - joined(3), joined(1) - joined(4)]
    edges = (row == 0).astype(F32) + (row == rows - 1).astype(F32)
    scale = 1.0 / (1.0 + (4.0 - edges) * warmth)
    out = []
    for residual in residuals:
        value = residual * scale
        for _ in range(JAC):
            around = pltpu.roll(value, 1, 1) + pltpu.roll(value, LANES - 1, 1)
            around = around + jnp.where(row == 0, 0.0, pltpu.roll(value, 1, 0))
            around = around + jnp.where(row == rows - 1, 0.0, pltpu.roll(value, rows - 1, 0))
            value = (residual + warmth * around) * scale
        out.append(pltpu.roll(value, LANES - 4, 1))
    return out


def per_device(
    wide, count,
    prior_population, speeds, jacobian, octant, collision, solid_mask, wall_state, inflow,
):
    columns, rows, width = prior_population.shape
    blocks = width // LANES
    group_size = blocks // 2
    groups = wide // group_size
    assert groups * group_size == wide and columns == 16
    shape = jax.ShapeDtypeStruct
    stays = pl.BlockSpec(memory_space=pltpu.HBM)

    def tiles(*lead):
        return pltpu.VMEM(lead + (rows, LANES), F32)

    def dma(*counts):
        return pltpu.SemaphoreType.DMA(counts)

    arguments = [
        pltpu.with_memory_space_constraint(value, pltpu.HBM)
        for value in (
            octant, speeds, jacobian.reshape(1, width), wall_state.reshape(1, width),
            collision.T, solid_mask.T, inflow, prior_population,
        )
    ]
    return pl.pallas_call(
        functools.partial(fused_kernel, wide, count, group_size),
        out_shape=shape((columns, rows, width), F32),
        in_specs=[stays] * 8,
        out_specs=pl.BlockSpec(memory_space=pltpu.VMEM),
        scratch_shapes=[
            pltpu.SMEM((blocks,), jnp.int32),
            pltpu.VMEM((3, width), F32),
            pltpu.VMEM((1, width), F32),
            pltpu.VMEM((1, width), F32),
            pltpu.VMEM((rows, columns), F32),
            pltpu.VMEM((rows, columns), jnp.int32),
            pltpu.VMEM((2, rows, 2 * LANES), F32),
            pltpu.VMEM((columns, rows, width), F32),
            tiles(7, blocks),
            tiles(MOMENTS, blocks),
            tiles(columns, MOMENTS),
            tiles(2, columns),
            tiles(blocks, columns),
            tiles(blocks, columns),
            tiles(blocks, columns),
            tiles(blocks, columns),
            tiles(blocks, columns),
            tiles(8, columns),
            tiles(5),
            tiles(3),
            pltpu.VMEM((rows, 2 * LANES), F32),
            pltpu.VMEM((count, rows, 2 * LANES), F32),
            pltpu.VMEM((group_size, 2 * rows + 1, LANES), F32),
            pltpu.VMEM((group_size, 2 * rows + 1, LANES), F32),
            tiles(group_size),
            tiles(2, 2, group_size),
            tiles(4),
            tiles(groups, 4),
            tiles(group_size, 2),
            tiles(group_size, 2),
            tiles(),
            tiles(3, count),
            dma(7), dma(CHUNKS), dma(count), dma(count), dma(group_size), dma(group_size),
            dma(groups), dma(groups), dma(group_size), dma(group_size),
            dma(3, count), dma(3, count),
        ],
        compiler_params=pltpu.CompilerParams(
            collective_id=0, has_side_effects=True, vmem_limit_bytes=40 * 1024 * 1024
        ),
    )(*arguments)


def solution(mesh):
    in_specs = (
        P("gx", None, "vert"),
        P(None, "vert"),
        P("vert"),
        P("vert"),
        P("gx", None),
        P("gx", None),
        P("vert"),
        P(None, None, "vert"),
    )
    return jax.shard_map(
        functools.partial(per_device, mesh.shape["gx"], mesh.shape["vert"]),
        mesh=mesh,
        in_specs=in_specs,
        out_specs=P("gx", None, "vert"),
        check_vma=False,
    )
```

```python
import functools
import math

import jax
import jax.numpy as jnp
from jax import lax
from jax.experimental import pallas as pl
from jax.experimental.pallas import tpu as pltpu
from jax.sharding import PartitionSpec as P

VEL = 32768
LANES = 128
JAC = 4
CHUNKS = 4
MOMENTS = 13
SOLID_DEPTH = 60.0
LOG_SPAN = 2.0 * math.log(60.0)
F32 = jnp.float32
MESH = pl.DeviceIdType.MESH

CX, CY, CZ, WEIGHT, WEIGHT_E, NEG_INV, WALL = range(7)


def lane_block(index):
    return pl.ds(pl.multiple_of(index * LANES, LANES), LANES)


def lane_index(rows):
    return lax.broadcasted_iota(jnp.int32, (rows, LANES), 1)


def row_index(rows):
    return lax.broadcasted_iota(jnp.int32, (rows, LANES), 0)


def velocity(speeds_ref, octant, block, rows):
    signs = (
        1 - 2 * lax.rem(octant, 2),
        1 - 2 * lax.rem(lax.div(octant, 2), 2),
        1 - 2 * lax.div(octant, 4),
    )
    return [
        jnp.broadcast_to(speeds_ref[n : n + 1, lane_block(block)], (rows, LANES)) * sign.astype(F32)
        for n, sign in enumerate(signs)
    ]


def cell_values(low, high):
    picked = []
    for m in range(MOMENTS):
        source = low if m < 8 else high
        shift = (LANES - 16 * (m % 8)) % LANES
        picked.append(pltpu.roll(source, shift, 1) if shift else source)
    valid = lane_index(low.shape[0]) < 16
    rho, sx, sy, sz, pxx, pxy, pxz, pyy, pyz, pzz, qx, qy, qz = (
        jnp.where(valid, value, 1.0) for value in picked
    )
    ux, uy, uz = sx / rho, sy / rho, sz / rho
    flow_sq = ux * ux + uy * uy + uz * uz
    second = pxx + pyy + pzz
    warmth = (second / rho - flow_sq) / 3.0
    swirl = rho * flow_sq
    heat_x = 0.5 * (qx - second * ux) - (ux * pxx + uy * pxy + uz * pxz) + swirl * ux
    heat_y = 0.5 * (qy - second * uy) - (ux * pxy + uy * pyy + uz * pyz) + swirl * uy
    heat_z = 0.5 * (qz - second * uz) - (ux * pxz + uy * pyz + uz * pzz) + swirl * uz
    return {
        "rho": rho, "ux": ux, "uy": uy, "uz": uz, "flow_sq": flow_sq, "warmth": warmth,
        "energy": 0.5 * second, "hx": heat_x, "hy": heat_y, "hz": heat_z,
    }


def maxwell_scale(cell):
    area = (2.0 * math.pi) * cell["warmth"]
    return cell["rho"] / (area * jnp.sqrt(area))


def spread(value, column, rows):
    return jnp.broadcast_to(value[:, column : column + 1], (rows, LANES))


def fused_kernel(
    wide, count, group_size,
    octant_in, speeds_in, jacobian_in, wall_in, collision_in, solid_in, inflow_in, prior_in,
    out_ref,
    octant_ref, speeds_ref, jacobian_ref, wall_ref, collision_ref, solid_ref, inflow_ref, prior,
    table, moment, totals, cells, att, decay, gain, power, bell, coef, extra, half_sums, tiles_ref,
    mine, vert_slots, message, arrived, depths, prefix, joint, joint_slots,
    result, incoming, tile, halo_slots,
    argument_sem, prior_sem, vert_send, vert_recv, out_send, out_recv, joint_send, joint_recv,
    back_send, back_recv, halo_send, halo_recv,
):
    columns, rows, width = out_ref.shape
    blocks = width // LANES
    groups = wide // group_size
    me = lax.axis_index("vert")
    col = lax.axis_index("gx")
    group, pos = lax.div(col, group_size), lax.rem(col, group_size)
    diagonal = lane_index(rows) == row_index(rows)
    part = columns // CHUNKS

    def prior_copy(c):
        span = pl.ds(c * part, part)
        return pltpu.make_async_copy(prior_in.at[span], prior.at[span], prior_sem.at[c])

    owned = pl.ds(pl.multiple_of(pos * (2 * LANES), 2 * LANES), 2 * LANES)
    pairs = (
        (octant_in, octant_ref), (speeds_in, speeds_ref), (jacobian_in, jacobian_ref),
        (wall_in, wall_ref), (collision_in, collision_ref), (solid_in, solid_ref),
        (inflow_in.at[:, :, owned], inflow_ref),
    )
    arguments = [
        pltpu.make_async_copy(source, target, argument_sem.at[n])
        for n, (source, target) in enumerate(pairs)
    ]
    for copy in arguments[:3]:
        copy.start()
    for c in range(CHUNKS):
        prior_copy(c).start()
    for copy in arguments[3:]:
        copy.start()

    def in_vert(k):
        return {"vert": lax.rem(me + k, count)}

    def in_group(p):
        return {"gx": group * group_size + p}

    def in_joint(g):
        return {"gx": g * group_size + pos}

    sides = [lax.rem(col + 1, wide), col, lax.rem(col + wide - 1, wide)]
    halo_partners = [(side, k) for side in (0, 1, 2) for k in range(count) if (side, k) != (1, 0)]

    def in_halo(side, k):
        return {"gx": sides[side], "vert": lax.rem(me + k, count)}

    barrier = pltpu.get_barrier_semaphore()

    def greet(device):
        pl.semaphore_signal(barrier, inc=1, device_id=device, device_id_type=MESH)

    for side, k in halo_partners:
        greet(in_halo(side, k))
    for k in range(1, group_size):
        greet(in_group(lax.rem(pos + k, group_size)))
    for k in range(1, groups):
        greet(in_joint(lax.rem(group + k, groups)))

    for copy in arguments[:3]:
        copy.wait()

    def build(b, carry):
        cx, cy, cz = velocity(speeds_ref, octant_ref[b], b, rows)
        sx, sy, sz = (
            jnp.broadcast_to(speeds_ref[n : n + 1, lane_block(b)], (rows, LANES)) for n in range(3)
        )
        jac = jnp.broadcast_to(jacobian_ref[:, lane_block(b)], (rows, LANES))
        w = jac * sx * sy * sz * (LOG_SPAN**3 / VEL)
        square = cx * cx + cy * cy + cz * cz
        wx, wy, wz = w * cx, w * cy, w * cz
        table[CX, b] = cx
        table[CY, b] = cy
        table[CZ, b] = cz
        table[WEIGHT, b] = w
        table[WEIGHT_E, b] = w * (0.5 * square)
        entries = (
            w, wx, wy, wz,
            wx * cx, wx * cy, wx * cz, wy * cy, wy * cz, wz * cz,
            wx * square, wy * square, wz * square,
        )
        for m, entry in enumerate(entries):
            moment[m, b] = entry
        return carry

    lax.fori_loop(0, blocks, build, 0)

    lane = lane_index(rows)

    zero_tile = jnp.zeros((rows, LANES), F32)

    def pair(g, carry):
        def add(b, sums):
            sums = list(sums)
            left = prior[2 * g, :, lane_block(b)]
            right = prior[2 * g + 1, :, lane_block(b)]
            for m in range(MOMENTS):
                entry = moment[m, b]
                sums[m] = sums[m] + left * entry
                sums[MOMENTS + m] = sums[MOMENTS + m] + right * entry
            return tuple(sums)

        sums = lax.fori_loop(0, blocks, add, (zero_tile,) * (2 * MOMENTS), unroll=4)
        for m in range(MOMENTS):
            totals[2 * g, m] = sums[m]
            totals[2 * g + 1, m] = sums[MOMENTS + m]
        return carry

    def moment_chunk(c, carry):
        prior_copy(c).wait()
        return lax.fori_loop(c * (part // 2), (c + 1) * (part // 2), pair, carry)

    lax.fori_loop(0, CHUNKS, moment_chunk, 0)

    def pack(c, packed):
        packed = list(packed)
        for n in range(part):
            for m in range(MOMENTS):
                total = jnp.sum(totals[c * part + n, m], axis=1, keepdims=True)
                spot = lane == (m % 8) * 16 + c * part + n
                packed[m // 8] = jnp.where(spot, total, packed[m // 8])
        return tuple(packed)

    low, high = lax.fori_loop(0, CHUNKS, pack, (zero_tile, zero_tile))
    mine[:, :LANES] = low
    mine[:, LANES:] = high

    pl.semaphore_wait(barrier, len(halo_partners) + group_size - 1 + groups - 1)

    def vert_copy(k, slot):
        return pltpu.make_async_remote_copy(
            src_ref=mine, dst_ref=vert_slots.at[slot],
            send_sem=vert_send.at[k], recv_sem=vert_recv.at[slot],
            device_id=in_vert(k), device_id_type=MESH,
        )

    for k in range(1, count):
        vert_copy(k, me).start()

    for copy in arguments[3:]:
        copy.wait()
    walled = solid_ref[...] == 1
    optical = jnp.where(walled, SOLID_DEPTH, collision_ref[...])
    flags = jnp.where(walled, 1.0, 0.0)
    total_depth = zero_tile
    for i in range(columns):
        cells[0, i] = spread(optical, i, rows)
        cells[1, i] = spread(flags, i, rows)
        total_depth = total_depth + cells[0, i]
    depth_row = jnp.sum(jnp.where(diagonal, total_depth, 0.0), axis=0, keepdims=True)

    def decays(b, carry):
        backward = lax.rem(octant_ref[b], 2)
        speed = jnp.broadcast_to(speeds_ref[0:1, lane_block(b)], (rows, LANES))
        neg_inv = -1.0 / speed
        table[NEG_INV, b] = neg_inv
        table[WALL, b] = jnp.broadcast_to(wall_ref[:, lane_block(b)], (rows, LANES))
        running = jnp.ones((rows, LANES), F32)
        for s in range(columns):
            one = jnp.exp(cells[0, s + backward * (columns - 1 - 2 * s)] * neg_inv)
            running = running * one
            att[b, s] = one
            decay[b, s] = running
        return carry

    lax.fori_loop(0, blocks, decays, 0)

    vert_slots[me] = mine[...]
    for k in range(1, count):
        vert_copy(k, lax.rem(me + k, count)).wait_recv()
    total = vert_slots[0]
    for k in range(1, count):
        total = total + vert_slots[k]
    cell = cell_values(total[:, :LANES], total[:, LANES:])
    warmth, rho = cell["warmth"], cell["rho"]
    scale = maxwell_scale(cell)
    factor = (-2.0 / 3.0) / (5.0 * rho * warmth * warmth)
    values = (
        cell["ux"], cell["uy"], cell["uz"], -0.5 / warmth, scale,
        cell["hx"] * factor, cell["hy"] * factor, cell["hz"] * factor,
    )
    for q, value in enumerate(values):
        for i in range(columns):
            coef[q, i] = spread(value, i, rows)
    packed = zero_tile
    for n, name in ((2, "warmth"), (3, "rho"), (4, "energy")):
        inside = jnp.logical_and(lane >= 16 * n, lane < 16 * n + 16)
        packed = jnp.where(inside, pltpu.roll(cell[name], 16 * n, 1), packed)
    extra[0] = packed
    for n, value in enumerate((rho, warmth, cell["flow_sq"], scale)):
        extra[1 + n] = value

    def out_copy(p, slot):
        return pltpu.make_async_remote_copy(
            src_ref=message.at[p], dst_ref=arrived.at[slot],
            send_sem=out_send.at[p], recv_sem=out_recv.at[slot],
            device_id=in_group(p), device_id_type=MESH,
        )

    def sweep(k, carry):
        p = lax.rem(pos + k, group_size)
        for q in range(2):
            b = 2 * p + q
            backward = lax.rem(octant_ref[b], 2)
            cx, cy, cz, wall = table[CX, b], table[CY, b], table[CZ, b], table[WALL, b]
            running = jnp.zeros((rows, LANES), F32)
            for s in range(columns):
                i = s + backward * (columns - 1 - 2 * s)
                px, py, pz = cx - coef[0, i], cy - coef[1, i], cz - coef[2, i]
                exponent = (px * px + py * py + pz * pz) * coef[3, i]
                skew = (px * coef[5, i] + py * coef[6, i] + pz * coef[7, i]) * (exponent + 2.5)
                weight = jnp.exp(exponent)
                power[b, s] = exponent
                bell[b, s] = weight
                target = coef[4, i] * weight * (1.0 + skew)
                source = jnp.where(cells[1, i] > 0.5, wall, target)
                one = att[b, s]
                running = one * running + (1.0 - one) * source
                gain[b, s] = running
            message[p, q * rows : (q + 1) * rows] = running
        message[p, 2 * rows : 2 * rows + 1] = depth_row

        @pl.when(k < group_size)
        def _():
            out_copy(p, pos).start()

        return carry

    lax.fori_loop(1, group_size + 1, sweep, 0)
    arrived[pos] = message[pos]

    def gain_sums(b, sums):
        backward = lax.rem(octant_ref[b], 2)
        weight, weight_e = table[WEIGHT, b], table[WEIGHT_E, b]
        sums = list(sums)
        for i in range(columns):
            value = gain[b, i + backward * (columns - 1 - 2 * i)]
            sums[i] = sums[i] + value * weight
            sums[columns + i] = sums[columns + i] + value * weight_e
        return tuple(sums)

    sums = lax.fori_loop(0, blocks, gain_sums, (zero_tile,) * (2 * columns))
    for n in range(2 * columns):
        half_sums[n] = sums[n]

    def wait_out(k, carry):
        out_copy(pos, lax.rem(pos + k, group_size)).wait_recv()
        return carry

    lax.fori_loop(1, group_size, wait_out, 0)

    for j in range(group_size):
        row = jnp.broadcast_to(arrived[j, 2 * rows : 2 * rows + 1], (rows, LANES))
        depth = jnp.sum(jnp.where(diagonal, row, 0.0), axis=1, keepdims=True)
        depths[j] = jnp.broadcast_to(depth, (rows, LANES))
    backwards = [lax.rem(octant_ref[2 * pos + q], 2) for q in range(2)]
    for q in range(2):
        neg_inv = table[NEG_INV, 2 * pos + q]
        kept, running = jnp.ones((rows, LANES), F32), jnp.zeros((rows, LANES), F32)
        for s in range(group_size):
            t = s + backwards[q] * (group_size - 1 - 2 * s)
            prefix[0, q, s] = kept
            prefix[1, q, s] = running
            one = jnp.exp(depths[t] * neg_inv)
            running = one * running + arrived[t, q * rows : (q + 1) * rows]
            kept = kept * one
        joint[q] = running
        joint[2 + q] = kept

    def joint_copy(g, slot):
        return pltpu.make_async_remote_copy(
            src_ref=joint, dst_ref=joint_slots.at[slot],
            send_sem=joint_send.at[g], recv_sem=joint_recv.at[slot],
            device_id=in_joint(g), device_id_type=MESH,
        )

    for k in range(1, groups):
        joint_copy(lax.rem(group + k, groups), group).start()
    joint_slots[group] = joint[...]
    for k in range(1, groups):
        joint_copy(group, lax.rem(group + k, groups)).wait_recv()
    entering = []
    for q in range(2):
        state = inflow_ref[backwards[q], :, q * LANES : (q + 1) * LANES]
        place = group + backwards[q] * (groups - 1 - 2 * group)
        for s in range(groups - 1):
            g = s + backwards[q] * (groups - 1 - 2 * s)
            before = jnp.broadcast_to((place - s).astype(F32), (rows, LANES)) > 0.5
            longer = joint_slots[g, 2 + q] * state + joint_slots[g, q]
            state = jnp.where(before, longer, state)
        entering.append(state)

    def back_copy(j, slot):
        return pltpu.make_async_remote_copy(
            src_ref=result.at[j], dst_ref=incoming.at[slot],
            send_sem=back_send.at[j], recv_sem=back_recv.at[slot],
            device_id=in_group(j), device_id_type=MESH,
        )

    def send_back(k, carry):
        j = lax.rem(pos + k, group_size)
        for q in range(2):
            s = j + backwards[q] * (group_size - 1 - 2 * j)
            result[j, q] = prefix[0, q, s] * carry[q] + prefix[1, q, s]

        @pl.when(k < group_size)
        def _():
            back_copy(j, pos).start()

        return carry

    lax.fori_loop(1, group_size + 1, send_back, tuple(entering))
    incoming[pos] = result[pos]

    def halves(k, sums):
        p = lax.rem(pos + group_size - k, group_size)

        @pl.when(k > 0)
        def _():
            back_copy(pos, p).wait_recv()

        sums = list(sums)
        for q in range(2):
            b = 2 * p + q
            backward = lax.rem(octant_ref[b], 2)
            weight, weight_e = table[WEIGHT, b], table[WEIGHT_E, b]
            enter = incoming[p, q]
            for i in range(columns):
                s = i + backward * (columns - 1 - 2 * i)
                value = decay[b, s] * enter
                sums[i] = sums[i] + value * weight
                sums[columns + i] = sums[columns + i] + value * weight_e
        return tuple(sums)

    sums = tuple(half_sums[n] for n in range(2 * columns))
    sums = lax.fori_loop(0, group_size, halves, sums)
    packed = extra[0]
    for n in range(2 * columns):
        packed = jnp.where(lane == n, jnp.sum(sums[n], axis=1, keepdims=True), packed)
    tile[...] = packed

    def halo_copy(side, k, slot):
        return pltpu.make_async_remote_copy(
            src_ref=tile, dst_ref=halo_slots.at[side, slot],
            send_sem=halo_send.at[side, k], recv_sem=halo_recv.at[side, slot],
            device_id=in_halo(side, k), device_id_type=MESH,
        )

    for side, k in halo_partners:
        halo_copy(side, k, me).start()
    halo_slots[1, me] = tile[...]

    def form(b, carry):
        backward = lax.rem(octant_ref[b], 2)
        enter = incoming[lax.div(b, 2), lax.rem(b, 2)]
        for i in range(columns):
            s = i + backward * (columns - 1 - 2 * i)
            out_ref[i, :, lane_block(b)] = decay[b, s] * enter + gain[b, s]
        return carry

    lax.fori_loop(0, blocks, form, 0)

    for k in range(1, count):
        vert_copy(k, me).wait_send()
    for k in range(1, groups):
        joint_copy(lax.rem(group + k, groups), group).wait_send()

    def finish_sends(k, carry):
        p = lax.rem(pos + k, group_size)
        out_copy(p, pos).wait_send()
        back_copy(p, pos).wait_send()
        return carry

    lax.fori_loop(1, group_size, finish_sends, 0)
    for side, k in halo_partners:
        halo_copy(side, k, me).wait_send()

    for side, k in halo_partners:
        halo_copy(side, k, lax.rem(me + k, count)).wait_recv()
    for side in range(3):
        total = halo_slots[side, 0]
        for k in range(1, count):
            total = total + halo_slots[side, k]
        total = jnp.where(lane < 2 * columns, total, halo_slots[side, 0])
        if side == 0:
            total = jnp.where(col == 0, 0.0, total)
        if side == 2:
            total = jnp.where(col == wide - 1, 0.0, total)
        tiles_ref[side] = total

    rho, warmth, flow_sq, scale = (extra[1 + n] for n in range(4))
    change_rho, change_energy = corrections(tiles_ref)
    change_warmth = (2.0 * change_energy / 3.0 - (warmth + flow_sq / 3.0) * change_rho) / rho
    ratio_rho = change_rho / rho
    ratio_warmth = change_warmth / warmth
    level, slope = scale * (ratio_rho - 1.5 * ratio_warmth), -(scale * ratio_warmth)

    def finish_columns(low, high):
        levels = [spread(level, i, rows) for i in range(low, high)]
        slopes = [spread(slope, i, rows) for i in range(low, high)]

        def finish(b, carry):
            backward = lax.rem(octant_ref[b], 2)
            for n, i in enumerate(range(low, high)):
                s = i + backward * (columns - 1 - 2 * i)
                change = bell[b, s] * (levels[n] + slopes[n] * power[b, s])
                out_ref[i, :, lane_block(b)] = out_ref[i, :, lane_block(b)] + change
            return carry

        lax.fori_loop(0, blocks, finish, 0)

    finish_columns(0, columns // 2)
    finish_columns(columns // 2, columns)


def corrections(tiles_ref):
    rows = tiles_ref.shape[1]
    lane, row = lane_index(rows), row_index(rows)

    def joined(n):
        def moved(side, start, place):
            shift = (place - 16 * n - start) % LANES
            return pltpu.roll(tiles_ref[side], shift, 1) if shift else tiles_ref[side]

        value = jnp.where(lane < 4, moved(0, 12, 0), moved(1, 0, 4))
        value = jnp.where(lane < 20, value, moved(2, 0, 20))
        return jnp.where(lane < 24, value, 0.0)

    warmth = joined(2)
    residuals = [joined(0) - joined(3), joined(1) - joined(4)]
    edges = (row == 0).astype(F32) + (row == rows - 1).astype(F32)
    scale = 1.0 / (1.0 + (4.0 - edges) * warmth)
    out = []
    for residual in residuals:
        value = residual * scale
        for _ in range(JAC):
            around = pltpu.roll(value, 1, 1) + pltpu.roll(value, LANES - 1, 1)
            around = around + jnp.where(row == 0, 0.0, pltpu.roll(value, 1, 0))
            around = around + jnp.where(row == rows - 1, 0.0, pltpu.roll(value, rows - 1, 0))
            value = (residual + warmth * around) * scale
        out.append(pltpu.roll(value, LANES - 4, 1))
    return out


def per_device(
    wide, count,
    prior_population, speeds, jacobian, octant, collision, solid_mask, wall_state, inflow,
):
    columns, rows, width = prior_population.shape
    blocks = width // LANES
    group_size = blocks // 2
    groups = wide // group_size
    assert groups * group_size == wide and columns == 16
    shape = jax.ShapeDtypeStruct
    stays = pl.BlockSpec(memory_space=pltpu.HBM)

    def tiles(*lead):
        return pltpu.VMEM(lead + (rows, LANES), F32)

    def dma(*counts):
        return pltpu.SemaphoreType.DMA(counts)

    arguments = [
        pltpu.with_memory_space_constraint(value, pltpu.HBM)
        for value in (
            octant, speeds, jacobian.reshape(1, width), wall_state.reshape(1, width),
            collision.T, solid_mask.T, inflow, prior_population,
        )
    ]
    return pl.pallas_call(
        functools.partial(fused_kernel, wide, count, group_size),
        out_shape=shape((columns, rows, width), F32),
        in_specs=[stays] * 8,
        out_specs=pl.BlockSpec(memory_space=pltpu.VMEM),
        scratch_shapes=[
            pltpu.SMEM((blocks,), jnp.int32),
            pltpu.VMEM((3, width), F32),
            pltpu.VMEM((1, width), F32),
            pltpu.VMEM((1, width), F32),
            pltpu.VMEM((rows, columns), F32),
            pltpu.VMEM((rows, columns), jnp.int32),
            pltpu.VMEM((2, rows, 2 * LANES), F32),
            pltpu.VMEM((columns, rows, width), F32),
            tiles(7, blocks),
            tiles(MOMENTS, blocks),
            tiles(columns, MOMENTS),
            tiles(2, columns),
            tiles(blocks, columns),
            tiles(blocks, columns),
            tiles(blocks, columns),
            tiles(blocks, columns),
            tiles(blocks, columns),
            tiles(8, columns),
            tiles(5),
            tiles(2 * columns),
            tiles(3),
            pltpu.VMEM((rows, 2 * LANES), F32),
            pltpu.VMEM((count, rows, 2 * LANES), F32),
            pltpu.VMEM((group_size, 2 * rows + 1, LANES), F32),
            pltpu.VMEM((group_size, 2 * rows + 1, LANES), F32),
            tiles(group_size),
            tiles(2, 2, group_size),
            tiles(4),
            tiles(groups, 4),
            tiles(group_size, 2),
            tiles(group_size, 2),
            tiles(),
            tiles(3, count),
            dma(7), dma(CHUNKS), dma(count), dma(count), dma(group_size), dma(group_size),
            dma(groups), dma(groups), dma(group_size), dma(group_size),
            dma(3, count), dma(3, count),
        ],
        compiler_params=pltpu.CompilerParams(
            collective_id=0, has_side_effects=True, vmem_limit_bytes=40 * 1024 * 1024
        ),
    )(*arguments)


def solution(mesh):
    in_specs = (
        P("gx", None, "vert"),
        P(None, "vert"),
        P("vert"),
        P("vert"),
        P("gx", None),
        P("gx", None),
        P("vert"),
        P(None, None, "vert"),
    )
    return jax.shard_map(
        functools.partial(per_device, mesh.shape["gx"], mesh.shape["vert"]),
        mesh=mesh,
        in_specs=in_specs,
        out_specs=P("gx", None, "vert"),
        check_vma=False,
    )
```

```python
import functools
import math

import jax
import jax.numpy as jnp
from jax import lax
from jax.experimental import pallas as pl
from jax.experimental.pallas import tpu as pltpu
from jax.sharding import PartitionSpec as P

VEL = 32768
LANES = 128
JAC = 4
CHUNKS = 4
MOMENTS = 13
SOLID_DEPTH = 60.0
LOG_SPAN = 2.0 * math.log(60.0)
F32 = jnp.float32
MESH = pl.DeviceIdType.MESH

CX, CY, CZ, WEIGHT, WEIGHT_E, NEG_INV, WALL = range(7)


def lane_block(index):
    return pl.ds(pl.multiple_of(index * LANES, LANES), LANES)


def lane_index(rows):
    return lax.broadcasted_iota(jnp.int32, (rows, LANES), 1)


def row_index(rows):
    return lax.broadcasted_iota(jnp.int32, (rows, LANES), 0)


def velocity(speeds_ref, octant, block, rows):
    signs = (
        1 - 2 * lax.rem(octant, 2),
        1 - 2 * lax.rem(lax.div(octant, 2), 2),
        1 - 2 * lax.div(octant, 4),
    )
    return [
        jnp.broadcast_to(speeds_ref[n : n + 1, lane_block(block)], (rows, LANES)) * sign.astype(F32)
        for n, sign in enumerate(signs)
    ]


def cell_values(low, high):
    picked = []
    for m in range(MOMENTS):
        source = low if m < 8 else high
        shift = (LANES - 16 * (m % 8)) % LANES
        picked.append(pltpu.roll(source, shift, 1) if shift else source)
    valid = lane_index(low.shape[0]) < 16
    rho, sx, sy, sz, pxx, pxy, pxz, pyy, pyz, pzz, qx, qy, qz = (
        jnp.where(valid, value, 1.0) for value in picked
    )
    ux, uy, uz = sx / rho, sy / rho, sz / rho
    flow_sq = ux * ux + uy * uy + uz * uz
    second = pxx + pyy + pzz
    warmth = (second / rho - flow_sq) / 3.0
    swirl = rho * flow_sq
    heat_x = 0.5 * (qx - second * ux) - (ux * pxx + uy * pxy + uz * pxz) + swirl * ux
    heat_y = 0.5 * (qy - second * uy) - (ux * pxy + uy * pyy + uz * pyz) + swirl * uy
    heat_z = 0.5 * (qz - second * uz) - (ux * pxz + uy * pyz + uz * pzz) + swirl * uz
    return {
        "rho": rho, "ux": ux, "uy": uy, "uz": uz, "flow_sq": flow_sq, "warmth": warmth,
        "energy": 0.5 * second, "hx": heat_x, "hy": heat_y, "hz": heat_z,
    }


def maxwell_scale(cell):
    area = (2.0 * math.pi) * cell["warmth"]
    return cell["rho"] / (area * jnp.sqrt(area))


def spread(value, column, rows):
    return jnp.broadcast_to(value[:, column : column + 1], (rows, LANES))


def fused_kernel(
    wide, count, group_size,
    octant_in, speeds_in, jacobian_in, wall_in, collision_in, solid_in, inflow_in, prior_in,
    out_ref,
    octant_ref, speeds_ref, jacobian_ref, wall_ref, collision_ref, solid_ref, inflow_ref, prior,
    table, moment, totals, cells, att, decay, gain, power, bell, coef, extra, half_sums, tiles_ref,
    mine, vert_slots, message, arrived, depths, prefix, joint, joint_slots,
    result, incoming, tile, tile_slots, line_slots,
    argument_sem, prior_sem, vert_send, vert_recv, out_send, out_recv, joint_send, joint_recv,
    back_send, back_recv, tile_send, tile_recv, line_send, line_recv,
):
    columns, rows, width = out_ref.shape
    blocks = width // LANES
    groups = wide // group_size
    own = blocks // group_size
    me = lax.axis_index("vert")
    col = lax.axis_index("gx")
    group, pos = lax.div(col, group_size), lax.rem(col, group_size)
    diagonal = lane_index(rows) == row_index(rows)
    part = columns // CHUNKS

    def prior_copy(c):
        span = pl.ds(c * part, part)
        return pltpu.make_async_copy(prior_in.at[span], prior.at[span], prior_sem.at[c])

    owned = pl.ds(pl.multiple_of(pos * (own * LANES), LANES), own * LANES)
    pairs = (
        (octant_in, octant_ref), (speeds_in, speeds_ref), (jacobian_in, jacobian_ref),
        (wall_in, wall_ref), (collision_in, collision_ref), (solid_in, solid_ref),
        (inflow_in.at[:, :, owned], inflow_ref),
    )
    arguments = [
        pltpu.make_async_copy(source, target, argument_sem.at[n])
        for n, (source, target) in enumerate(pairs)
    ]
    for copy in arguments[:3]:
        copy.start()
    for c in range(CHUNKS):
        prior_copy(c).start()
    for copy in arguments[3:]:
        copy.start()

    def in_vert(k):
        return {"vert": lax.rem(me + k, count)}

    def in_group(k):
        return {"gx": group * group_size + lax.rem(pos + k, group_size)}

    def in_joint(k):
        return {"gx": lax.rem(group + k, groups) * group_size + pos}

    def in_line(k):
        return {"gx": lax.rem(col + k, wide)}

    def send_to(k, source, slots, send_sem, recv_sem, device):
        pltpu.make_async_remote_copy(
            src_ref=source, dst_ref=slots.at[k - 1], send_sem=send_sem, recv_sem=recv_sem,
            device_id=device(k), device_id_type=MESH,
        ).start()

    def all_copies(copies, slots, send_sem, recv_sem, device):
        span = slots.at[pl.ds(0, copies)]
        return pltpu.make_async_remote_copy(
            src_ref=span, dst_ref=span, send_sem=send_sem, recv_sem=recv_sem,
            device_id=device(1), device_id_type=MESH,
        )

    def slot_of(sender, mine, size):
        return lax.rem(mine - sender - 1 + size, size)

    barrier = pltpu.get_barrier_semaphore()
    partners = [in_vert(k) for k in range(1, count)]
    partners += [in_group(k) for k in range(1, group_size)]
    partners += [in_joint(k) for k in range(1, groups)]
    partners += [in_line(1), in_line(wide - 1)]
    for device in partners:
        pl.semaphore_signal(barrier, inc=1, device_id=device, device_id_type=MESH)

    for copy in arguments[:3]:
        copy.wait()

    def build(b, carry):
        cx, cy, cz = velocity(speeds_ref, octant_ref[b], b, rows)
        sx, sy, sz = (
            jnp.broadcast_to(speeds_ref[n : n + 1, lane_block(b)], (rows, LANES)) for n in range(3)
        )
        jac = jnp.broadcast_to(jacobian_ref[:, lane_block(b)], (rows, LANES))
        w = jac * sx * sy * sz * (LOG_SPAN**3 / VEL)
        square = cx * cx + cy * cy + cz * cz
        wx, wy, wz = w * cx, w * cy, w * cz
        table[CX, b] = cx
        table[CY, b] = cy
        table[CZ, b] = cz
        table[WEIGHT, b] = w
        table[WEIGHT_E, b] = w * (0.5 * square)
        entries = (
            w, wx, wy, wz,
            wx * cx, wx * cy, wx * cz, wy * cy, wy * cz, wz * cz,
            wx * square, wy * square, wz * square,
        )
        for m, entry in enumerate(entries):
            moment[m, b] = entry
        return carry

    lax.fori_loop(0, blocks, build, 0)

    lane = lane_index(rows)

    zero_tile = jnp.zeros((rows, LANES), F32)

    def pair(g, carry):
        def add(b, sums):
            sums = list(sums)
            left = prior[2 * g, :, lane_block(b)]
            right = prior[2 * g + 1, :, lane_block(b)]
            for m in range(MOMENTS):
                entry = moment[m, b]
                sums[m] = sums[m] + left * entry
                sums[MOMENTS + m] = sums[MOMENTS + m] + right * entry
            return tuple(sums)

        sums = lax.fori_loop(0, blocks, add, (zero_tile,) * (2 * MOMENTS), unroll=4)
        for m in range(MOMENTS):
            totals[2 * g, m] = sums[m]
            totals[2 * g + 1, m] = sums[MOMENTS + m]
        return carry

    def moment_chunk(c, carry):
        prior_copy(c).wait()
        return lax.fori_loop(c * (part // 2), (c + 1) * (part // 2), pair, carry)

    lax.fori_loop(0, CHUNKS, moment_chunk, 0)

    def pack(c, packed):
        packed = list(packed)
        for n in range(part):
            for m in range(MOMENTS):
                total = jnp.sum(totals[c * part + n, m], axis=1, keepdims=True)
                spot = lane == (m % 8) * 16 + c * part + n
                packed[m // 8] = jnp.where(spot, total, packed[m // 8])
        return tuple(packed)

    low, high = lax.fori_loop(0, CHUNKS, pack, (zero_tile, zero_tile))
    mine[:, :LANES] = low
    mine[:, LANES:] = high

    pl.semaphore_wait(barrier, len(partners))

    for k in range(1, count):
        send_to(k, mine, vert_slots, vert_send, vert_recv, in_vert)

    for copy in arguments[3:]:
        copy.wait()
    walled = solid_ref[...] == 1
    optical = jnp.where(walled, SOLID_DEPTH, collision_ref[...])
    flags = jnp.where(walled, 1.0, 0.0)
    total_depth = zero_tile
    for i in range(columns):
        cells[0, i] = spread(optical, i, rows)
        cells[1, i] = spread(flags, i, rows)
        total_depth = total_depth + cells[0, i]
    depth_row = jnp.sum(jnp.where(diagonal, total_depth, 0.0), axis=0, keepdims=True)

    def decays(b, carry):
        backward = lax.rem(octant_ref[b], 2)
        speed = jnp.broadcast_to(speeds_ref[0:1, lane_block(b)], (rows, LANES))
        neg_inv = -1.0 / speed
        table[NEG_INV, b] = neg_inv
        table[WALL, b] = jnp.broadcast_to(wall_ref[:, lane_block(b)], (rows, LANES))
        running = jnp.ones((rows, LANES), F32)
        for s in range(columns):
            one = jnp.exp(cells[0, s + backward * (columns - 1 - 2 * s)] * neg_inv)
            running = running * one
            att[b, s] = one
            decay[b, s] = running
        return carry

    lax.fori_loop(0, blocks, decays, 0)

    total = mine[...]
    vert_copies = all_copies(count - 1, vert_slots, vert_send, vert_recv, in_vert)
    vert_copies.wait_recv()
    for k in range(count - 1):
        total = total + vert_slots[k]
    cell = cell_values(total[:, :LANES], total[:, LANES:])
    warmth, rho = cell["warmth"], cell["rho"]
    scale = maxwell_scale(cell)
    factor = (-2.0 / 3.0) / (5.0 * rho * warmth * warmth)
    values = (
        cell["ux"], cell["uy"], cell["uz"], -0.5 / warmth, scale,
        cell["hx"] * factor, cell["hy"] * factor, cell["hz"] * factor,
    )
    for q, value in enumerate(values):
        for i in range(columns):
            coef[q, i] = spread(value, i, rows)
    packed = zero_tile
    for n, name in ((2, "warmth"), (3, "rho"), (4, "energy")):
        inside = jnp.logical_and(lane >= 16 * n, lane < 16 * n + 16)
        packed = jnp.where(inside, pltpu.roll(cell[name], 16 * n, 1), packed)
    extra[0] = packed
    for n, value in enumerate((rho, warmth, cell["flow_sq"], scale)):
        extra[1 + n] = value

    def sweep(k, carry):
        p = lax.rem(pos + k, group_size)
        for q in range(own):
            b = own * p + q
            backward = lax.rem(octant_ref[b], 2)
            cx, cy, cz, wall = table[CX, b], table[CY, b], table[CZ, b], table[WALL, b]
            running = jnp.zeros((rows, LANES), F32)
            for s in range(columns):
                i = s + backward * (columns - 1 - 2 * s)
                px, py, pz = cx - coef[0, i], cy - coef[1, i], cz - coef[2, i]
                exponent = (px * px + py * py + pz * pz) * coef[3, i]
                skew = (px * coef[5, i] + py * coef[6, i] + pz * coef[7, i]) * (exponent + 2.5)
                weight = jnp.exp(exponent)
                power[b, s] = exponent
                bell[b, s] = weight
                target = coef[4, i] * weight * (1.0 + skew)
                source = jnp.where(cells[1, i] > 0.5, wall, target)
                one = att[b, s]
                running = one * running + (1.0 - one) * source
                gain[b, s] = running
            message[k - 1, q * rows : (q + 1) * rows] = running
        message[k - 1, own * rows : own * rows + 1] = depth_row

        @pl.when(k < group_size)
        def _():
            send_to(k, message.at[k - 1], arrived, out_send, out_recv, in_group)

        return carry

    lax.fori_loop(1, group_size + 1, sweep, 0)
    arrived[group_size - 1] = message[group_size - 1]

    def gain_sums(b, sums):
        backward = lax.rem(octant_ref[b], 2)
        weight, weight_e = table[WEIGHT, b], table[WEIGHT_E, b]
        sums = list(sums)
        for i in range(columns):
            value = gain[b, i + backward * (columns - 1 - 2 * i)]
            sums[i] = sums[i] + value * weight
            sums[columns + i] = sums[columns + i] + value * weight_e
        return tuple(sums)

    sums = lax.fori_loop(0, blocks, gain_sums, (zero_tile,) * (2 * columns))
    for n in range(2 * columns):
        half_sums[n] = sums[n]

    out_copies = all_copies(group_size - 1, arrived, out_send, out_recv, in_group)
    out_copies.wait_recv()

    group_depth = zero_tile
    for j in range(group_size):
        row = jnp.broadcast_to(arrived[j, own * rows : own * rows + 1], (rows, LANES))
        depth = jnp.sum(jnp.where(diagonal, row, 0.0), axis=1, keepdims=True)
        depths[j] = jnp.broadcast_to(depth, (rows, LANES))
        group_depth = group_depth + depths[j]
    backwards = [lax.rem(octant_ref[own * pos + q], 2) for q in range(own)]
    for q in range(own):
        neg_inv = table[NEG_INV, own * pos + q]
        kept, running = jnp.ones((rows, LANES), F32), zero_tile
        for s in range(group_size):
            t = slot_of(s + backwards[q] * (group_size - 1 - 2 * s), pos, group_size)
            prefix[0, q, s] = kept
            prefix[1, q, s] = running
            one = jnp.exp(depths[t] * neg_inv)
            running = one * running + arrived[t, q * rows : (q + 1) * rows]
            kept = kept * one
        joint[q] = running
    joint[own] = group_depth

    for k in range(1, groups):
        send_to(k, joint, joint_slots, joint_send, joint_recv, in_joint)
    joint_slots[groups - 1] = joint[...]
    joint_copies = all_copies(groups - 1, joint_slots, joint_send, joint_recv, in_joint)
    joint_copies.wait_recv()
    entering = []
    for q in range(own):
        neg_inv = table[NEG_INV, own * pos + q]
        state = inflow_ref[backwards[q], :, q * LANES : (q + 1) * LANES]
        place = group + backwards[q] * (groups - 1 - 2 * group)
        for s in range(groups - 1):
            g = slot_of(s + backwards[q] * (groups - 1 - 2 * s), group, groups)
            before = jnp.broadcast_to((place - s).astype(F32), (rows, LANES)) > 0.5
            longer = jnp.exp(joint_slots[g, own] * neg_inv) * state + joint_slots[g, q]
            state = jnp.where(before, longer, state)
        entering.append(state)

    for k in range(1, group_size + 1):
        j = lax.rem(pos + k, group_size)
        for q in range(own):
            s = j + backwards[q] * (group_size - 1 - 2 * j)
            result[k - 1, q] = prefix[0, q, s] * entering[q] + prefix[1, q, s]
        if k < group_size:
            send_to(k, result.at[k - 1], incoming, back_send, back_recv, in_group)
    incoming[group_size - 1] = result[group_size - 1]
    back_copies = all_copies(group_size - 1, incoming, back_send, back_recv, in_group)
    back_copies.wait_recv()

    def entering_tile(b):
        return incoming[slot_of(lax.div(b, own), pos, group_size), lax.rem(b, own)]

    def halves(b, sums):
        sums = list(sums)
        backward = lax.rem(octant_ref[b], 2)
        weight, weight_e = table[WEIGHT, b], table[WEIGHT_E, b]
        enter = entering_tile(b)
        for i in range(columns):
            value = decay[b, i + backward * (columns - 1 - 2 * i)] * enter
            sums[i] = sums[i] + value * weight
            sums[columns + i] = sums[columns + i] + value * weight_e
        return tuple(sums)

    sums = tuple(half_sums[n] for n in range(2 * columns))
    sums = lax.fori_loop(0, blocks, halves, sums)
    packed = extra[0]
    for n in range(2 * columns):
        packed = jnp.where(lane == n, jnp.sum(sums[n], axis=1, keepdims=True), packed)
    tile[...] = packed

    for k in range(1, count):
        send_to(k, tile, tile_slots, tile_send, tile_recv, in_vert)

    def form(b, carry):
        backward = lax.rem(octant_ref[b], 2)
        enter = entering_tile(b)
        for i in range(columns):
            s = i + backward * (columns - 1 - 2 * i)
            out_ref[i, :, lane_block(b)] = decay[b, s] * enter + gain[b, s]
        return carry

    lax.fori_loop(0, blocks, form, 0)

    tile_copies = all_copies(count - 1, tile_slots, tile_send, tile_recv, in_vert)
    tile_copies.wait_recv()
    total = tile[...]
    for k in range(count - 1):
        total = total + tile_slots[k]
    tiles_ref[1] = jnp.where(lane < 2 * columns, total, packed)

    def line_copy(n, k):
        return pltpu.make_async_remote_copy(
            src_ref=tiles_ref.at[1], dst_ref=line_slots.at[n],
            send_sem=line_send.at[n], recv_sem=line_recv.at[n],
            device_id=in_line(k), device_id_type=MESH,
        )

    lines = [line_copy(0, 1), line_copy(1, wide - 1)]
    for copy in lines:
        copy.start()
    for copies in (vert_copies, out_copies, joint_copies, back_copies, tile_copies):
        copies.wait_send()
    for copy in lines:
        copy.wait()
    tiles_ref[0] = jnp.where(col == 0, 0.0, line_slots[0])
    tiles_ref[2] = jnp.where(col == wide - 1, 0.0, line_slots[1])

    rho, warmth, flow_sq, scale = (extra[1 + n] for n in range(4))
    change_rho, change_energy = corrections(tiles_ref)
    change_warmth = (2.0 * change_energy / 3.0 - (warmth + flow_sq / 3.0) * change_rho) / rho
    ratio_rho = change_rho / rho
    ratio_warmth = change_warmth / warmth
    level, slope = scale * (ratio_rho - 1.5 * ratio_warmth), -(scale * ratio_warmth)

    def finish_columns(low, high):
        levels = [spread(level, i, rows) for i in range(low, high)]
        slopes = [spread(slope, i, rows) for i in range(low, high)]

        def finish(b, carry):
            backward = lax.rem(octant_ref[b], 2)
            for n, i in enumerate(range(low, high)):
                s = i + backward * (columns - 1 - 2 * i)
                change = bell[b, s] * (levels[n] + slopes[n] * power[b, s])
                out_ref[i, :, lane_block(b)] = out_ref[i, :, lane_block(b)] + change
            return carry

        lax.fori_loop(0, blocks, finish, 0)

    finish_columns(0, columns // 2)
    finish_columns(columns // 2, columns)


def corrections(tiles_ref):
    rows = tiles_ref.shape[1]
    lane, row = lane_index(rows), row_index(rows)

    def joined(n):
        def moved(side, start, place):
            shift = (place - 16 * n - start) % LANES
            return pltpu.roll(tiles_ref[side], shift, 1) if shift else tiles_ref[side]

        value = jnp.where(lane < 4, moved(0, 12, 0), moved(1, 0, 4))
        value = jnp.where(lane < 20, value, moved(2, 0, 20))
        return jnp.where(lane < 24, value, 0.0)

    warmth = joined(2)
    residuals = [joined(0) - joined(3), joined(1) - joined(4)]
    edges = (row == 0).astype(F32) + (row == rows - 1).astype(F32)
    scale = 1.0 / (1.0 + (4.0 - edges) * warmth)
    out = []
    for residual in residuals:
        value = residual * scale
        for _ in range(JAC):
            around = pltpu.roll(value, 1, 1) + pltpu.roll(value, LANES - 1, 1)
            around = around + jnp.where(row == 0, 0.0, pltpu.roll(value, 1, 0))
            around = around + jnp.where(row == rows - 1, 0.0, pltpu.roll(value, rows - 1, 0))
            value = (residual + warmth * around) * scale
        out.append(pltpu.roll(value, LANES - 4, 1))
    return out


def per_device(
    wide, count,
    prior_population, speeds, jacobian, octant, collision, solid_mask, wall_state, inflow,
):
    columns, rows, width = prior_population.shape
    blocks = width // LANES
    group_size = math.isqrt(wide)
    own = blocks // group_size
    groups = wide // group_size
    assert groups * group_size == wide and own * group_size == blocks and columns == 16
    shape = jax.ShapeDtypeStruct
    stays = pl.BlockSpec(memory_space=pltpu.HBM)

    def tiles(*lead):
        return pltpu.VMEM(lead + (rows, LANES), F32)

    def dma(*counts):
        return pltpu.SemaphoreType.DMA(counts)

    arguments = [
        pltpu.with_memory_space_constraint(value, pltpu.HBM)
        for value in (
            octant, speeds, jacobian.reshape(1, width), wall_state.reshape(1, width),
            collision.T, solid_mask.T, inflow, prior_population,
        )
    ]
    return pl.pallas_call(
        functools.partial(fused_kernel, wide, count, group_size),
        out_shape=shape((columns, rows, width), F32),
        in_specs=[stays] * 8,
        out_specs=pl.BlockSpec(memory_space=pltpu.VMEM),
        scratch_shapes=[
            pltpu.SMEM((blocks,), jnp.int32),
            pltpu.VMEM((3, width), F32),
            pltpu.VMEM((1, width), F32),
            pltpu.VMEM((1, width), F32),
            pltpu.VMEM((rows, columns), F32),
            pltpu.VMEM((rows, columns), jnp.int32),
            pltpu.VMEM((2, rows, own * LANES), F32),
            pltpu.VMEM((columns, rows, width), F32),
            tiles(7, blocks),
            tiles(MOMENTS, blocks),
            tiles(columns, MOMENTS),
            tiles(2, columns),
            tiles(blocks, columns),
            tiles(blocks, columns),
            tiles(blocks, columns),
            tiles(blocks, columns),
            tiles(blocks, columns),
            tiles(8, columns),
            tiles(5),
            tiles(2 * columns),
            tiles(3),
            pltpu.VMEM((rows, 2 * LANES), F32),
            pltpu.VMEM((count, rows, 2 * LANES), F32),
            pltpu.VMEM((group_size, own * rows + 1, LANES), F32),
            pltpu.VMEM((group_size, own * rows + 1, LANES), F32),
            tiles(group_size),
            tiles(2, own, group_size),
            tiles(own + 1),
            tiles(groups, own + 1),
            tiles(group_size, own),
            tiles(group_size, own),
            tiles(),
            tiles(count),
            tiles(2),
            dma(7), dma(CHUNKS),
        ] + [pltpu.SemaphoreType.DMA] * 10 + [
            dma(2), dma(2),
        ],
        compiler_params=pltpu.CompilerParams(
            collective_id=0, has_side_effects=True, vmem_limit_bytes=40 * 1024 * 1024
        ),
    )(*arguments)


def solution(mesh):
    in_specs = (
        P("gx", None, "vert"),
        P(None, "vert"),
        P("vert"),
        P("vert"),
        P("gx", None),
        P("gx", None),
        P("vert"),
        P(None, None, "vert"),
    )
    return jax.shard_map(
        functools.partial(per_device, mesh.shape["gx"], mesh.shape["vert"]),
        mesh=mesh,
        in_specs=in_specs,
        out_specs=P("gx", None, "vert"),
        check_vma=False,
    )
```

```python
import functools
import math

import jax
import jax.numpy as jnp
from jax import lax
from jax.experimental import pallas as pl
from jax.experimental.pallas import tpu as pltpu
from jax.sharding import PartitionSpec as P

VEL = 32768
LANES = 128
JAC = 4
CHUNKS = 4
MOMENTS = 13
SOLID_DEPTH = 60.0
LOG_SPAN = 2.0 * math.log(60.0)
F32 = jnp.float32
MESH = pl.DeviceIdType.MESH

CX, CY, CZ, WEIGHT, WEIGHT_E, NEG_INV, WALL = range(7)


def lane_block(index):
    return pl.ds(pl.multiple_of(index * LANES, LANES), LANES)


def lane_index(rows):
    return lax.broadcasted_iota(jnp.int32, (rows, LANES), 1)


def row_index(rows):
    return lax.broadcasted_iota(jnp.int32, (rows, LANES), 0)


def velocity(speeds_ref, octant, block, rows):
    signs = (
        1 - 2 * lax.rem(octant, 2),
        1 - 2 * lax.rem(lax.div(octant, 2), 2),
        1 - 2 * lax.div(octant, 4),
    )
    return [
        jnp.broadcast_to(speeds_ref[n : n + 1, lane_block(block)], (rows, LANES)) * sign.astype(F32)
        for n, sign in enumerate(signs)
    ]


def cell_values(low, high):
    picked = []
    for m in range(MOMENTS):
        source = low if m < 8 else high
        shift = (LANES - 16 * (m % 8)) % LANES
        picked.append(pltpu.roll(source, shift, 1) if shift else source)
    valid = lane_index(low.shape[0]) < 16
    rho, sx, sy, sz, pxx, pxy, pxz, pyy, pyz, pzz, qx, qy, qz = (
        jnp.where(valid, value, 1.0) for value in picked
    )
    ux, uy, uz = sx / rho, sy / rho, sz / rho
    flow_sq = ux * ux + uy * uy + uz * uz
    second = pxx + pyy + pzz
    warmth = (second / rho - flow_sq) / 3.0
    swirl = rho * flow_sq
    heat_x = 0.5 * (qx - second * ux) - (ux * pxx + uy * pxy + uz * pxz) + swirl * ux
    heat_y = 0.5 * (qy - second * uy) - (ux * pxy + uy * pyy + uz * pyz) + swirl * uy
    heat_z = 0.5 * (qz - second * uz) - (ux * pxz + uy * pyz + uz * pzz) + swirl * uz
    return {
        "rho": rho, "ux": ux, "uy": uy, "uz": uz, "flow_sq": flow_sq, "warmth": warmth,
        "energy": 0.5 * second, "hx": heat_x, "hy": heat_y, "hz": heat_z,
    }


def maxwell_scale(cell):
    area = (2.0 * math.pi) * cell["warmth"]
    return cell["rho"] / (area * jnp.sqrt(area))


def spread(value, column, rows):
    return jnp.broadcast_to(value[:, column : column + 1], (rows, LANES))


def fused_kernel(
    wide, count, group_size,
    octant_in, speeds_in, jacobian_in, wall_in, collision_in, solid_in, inflow_in, prior_in,
    out_ref,
    octant_ref, speeds_ref, jacobian_ref, wall_ref, collision_ref, solid_ref, inflow_ref, prior,
    table, moment, cells, att, decay, gain, power, bell, coef, extra, half_sums, tiles_ref,
    mine, vert_slots, message, arrived, depths, prefix, joint, joint_slots,
    result, incoming, tile, tile_slots, line_slots,
    argument_sem, prior_sem, vert_send, vert_recv, out_send, out_recv, joint_send, joint_recv,
    back_send, back_recv, tile_send, tile_recv, line_send, line_recv,
):
    columns, rows, width = out_ref.shape
    blocks = width // LANES
    groups = wide // group_size
    own = blocks // group_size
    me = lax.axis_index("vert")
    col = lax.axis_index("gx")
    group, pos = lax.div(col, group_size), lax.rem(col, group_size)
    diagonal = lane_index(rows) == row_index(rows)
    part = columns // CHUNKS

    def prior_copy(c):
        span = pl.ds(c * part, part)
        return pltpu.make_async_copy(prior_in.at[span], prior.at[span], prior_sem.at[c])

    owned = pl.ds(pl.multiple_of(pos * (own * LANES), LANES), own * LANES)
    pairs = (
        (octant_in, octant_ref), (speeds_in, speeds_ref), (jacobian_in, jacobian_ref),
        (wall_in, wall_ref), (collision_in, collision_ref), (solid_in, solid_ref),
        (inflow_in.at[:, :, owned], inflow_ref),
    )
    arguments = [
        pltpu.make_async_copy(source, target, argument_sem.at[n])
        for n, (source, target) in enumerate(pairs)
    ]
    for copy in arguments[:3]:
        copy.start()
    for c in range(CHUNKS):
        prior_copy(c).start()
    for copy in arguments[3:]:
        copy.start()

    def in_vert(k):
        return {"vert": lax.rem(me + k, count)}

    def in_group(k):
        return {"gx": group * group_size + lax.rem(pos + k, group_size)}

    def in_joint(k):
        return {"gx": lax.rem(group + k, groups) * group_size + pos}

    def in_line(side, k):
        step = (1, 0, wide - 1)[side]
        return {"gx": lax.rem(col + step, wide), "vert": lax.rem(me + k, count)}

    lines = [(side, k) for side in (0, 2) for k in range(count)]

    def send_to(k, source, slots, send_sem, recv_sem, device):
        pltpu.make_async_remote_copy(
            src_ref=source, dst_ref=slots.at[k - 1], send_sem=send_sem, recv_sem=recv_sem,
            device_id=device(k), device_id_type=MESH,
        ).start()

    def all_copies(copies, slots, send_sem, recv_sem, device):
        span = slots.at[pl.ds(0, copies)]
        return pltpu.make_async_remote_copy(
            src_ref=span, dst_ref=span, send_sem=send_sem, recv_sem=recv_sem,
            device_id=device(1), device_id_type=MESH,
        )

    def slot_of(sender, mine, size):
        return lax.rem(mine - sender - 1 + size, size)

    barrier = pltpu.get_barrier_semaphore()
    partners = [in_vert(k) for k in range(1, count)]
    partners += [in_group(k) for k in range(1, group_size)]
    partners += [in_joint(k) for k in range(1, groups)]
    partners += [in_line(side, k) for side, k in lines]
    for device in partners:
        pl.semaphore_signal(barrier, inc=1, device_id=device, device_id_type=MESH)

    for copy in arguments[:3]:
        copy.wait()

    moment[...] = jnp.zeros_like(moment)

    def build(b, carry):
        cx, cy, cz = velocity(speeds_ref, octant_ref[b], b, rows)
        sx, sy, sz = (
            jnp.broadcast_to(speeds_ref[n : n + 1, lane_block(b)], (rows, LANES)) for n in range(3)
        )
        jac = jnp.broadcast_to(jacobian_ref[:, lane_block(b)], (rows, LANES))
        w = jac * sx * sy * sz * (LOG_SPAN**3 / VEL)
        square = cx * cx + cy * cy + cz * cz
        wx, wy, wz = w * cx, w * cy, w * cz
        table[CX, b] = cx
        table[CY, b] = cy
        table[CZ, b] = cz
        table[WEIGHT, b] = w
        table[WEIGHT_E, b] = w * (0.5 * square)
        entries = (
            w, wx, wy, wz,
            wx * cx, wx * cy, wx * cz, wy * cy, wy * cz, wz * cz,
            wx * square, wy * square, wz * square,
        )
        for m, entry in enumerate(entries):
            moment[m : m + 1, lane_block(b)] = entry[0:1]
        return carry

    lax.fori_loop(0, blocks, build, 0)

    lane = lane_index(rows)

    zero_tile = jnp.zeros((rows, LANES), F32)

    moment_row = lax.broadcasted_iota(jnp.int32, (16, 2 * LANES), 0)
    place = lax.broadcasted_iota(jnp.int32, (16, 2 * LANES), 1)
    spaced = jnp.where(place == 16 * moment_row, 1.0, 0.0)
    for c in range(CHUNKS):
        prior_copy(c).wait()
    field = prior[...].reshape(columns * rows, width)
    product = lax.dot_general(
        field, moment[...], (((1,), (1,)), ((), ())),
        precision=lax.Precision.HIGHEST, preferred_element_type=F32,
    )
    product = jnp.dot(
        product, spaced, precision=lax.Precision.HIGHEST, preferred_element_type=F32
    )
    low, high = product[:rows, :LANES], product[:rows, LANES:]
    for i in range(1, columns):
        band = product[i * rows : (i + 1) * rows]
        low = low + pltpu.roll(band[:, :LANES], i, 1)
        high = high + pltpu.roll(band[:, LANES:], i, 1)
    mine[:, :LANES] = low
    mine[:, LANES:] = high

    pl.semaphore_wait(barrier, len(partners))

    for k in range(1, count):
        send_to(k, mine, vert_slots, vert_send, vert_recv, in_vert)

    for copy in arguments[3:]:
        copy.wait()
    walled = solid_ref[...] == 1
    optical = jnp.where(walled, SOLID_DEPTH, collision_ref[...])
    flags = jnp.where(walled, 1.0, 0.0)
    total_depth = zero_tile
    for i in range(columns):
        cells[0, i] = spread(optical, i, rows)
        cells[1, i] = spread(flags, i, rows)
        total_depth = total_depth + cells[0, i]
    depth_row = jnp.sum(jnp.where(diagonal, total_depth, 0.0), axis=0, keepdims=True)

    def decays(b, carry):
        backward = lax.rem(octant_ref[b], 2)
        speed = jnp.broadcast_to(speeds_ref[0:1, lane_block(b)], (rows, LANES))
        neg_inv = -1.0 / speed
        table[NEG_INV, b] = neg_inv
        table[WALL, b] = jnp.broadcast_to(wall_ref[:, lane_block(b)], (rows, LANES))
        running = jnp.ones((rows, LANES), F32)
        for s in range(columns):
            one = jnp.exp(cells[0, s + backward * (columns - 1 - 2 * s)] * neg_inv)
            running = running * one
            att[b, s] = one
            decay[b, s] = running
        return carry

    lax.fori_loop(0, blocks, decays, 0)

    total = mine[...]
    vert_copies = all_copies(count - 1, vert_slots, vert_send, vert_recv, in_vert)
    vert_copies.wait_recv()
    for k in range(count - 1):
        total = total + vert_slots[k]
    cell = cell_values(total[:, :LANES], total[:, LANES:])
    warmth, rho = cell["warmth"], cell["rho"]
    scale = maxwell_scale(cell)
    factor = (-2.0 / 3.0) / (5.0 * rho * warmth * warmth)
    values = (
        cell["ux"], cell["uy"], cell["uz"], -0.5 / warmth, scale,
        cell["hx"] * factor, cell["hy"] * factor, cell["hz"] * factor,
    )
    for q, value in enumerate(values):
        for i in range(columns):
            coef[q, i] = spread(value, i, rows)
    packed = zero_tile
    for n, name in ((2, "warmth"), (3, "rho"), (4, "energy")):
        inside = jnp.logical_and(lane >= 16 * n, lane < 16 * n + 16)
        packed = jnp.where(inside, pltpu.roll(cell[name], 16 * n, 1), packed)
    extra[0] = packed
    for n, value in enumerate((rho, warmth, cell["flow_sq"], scale)):
        extra[1 + n] = value

    def sweep(k, carry):
        p = lax.rem(pos + k, group_size)
        for q in range(own):
            b = own * p + q
            backward = lax.rem(octant_ref[b], 2)
            cx, cy, cz, wall = table[CX, b], table[CY, b], table[CZ, b], table[WALL, b]
            running = jnp.zeros((rows, LANES), F32)
            for s in range(columns):
                i = s + backward * (columns - 1 - 2 * s)
                px, py, pz = cx - coef[0, i], cy - coef[1, i], cz - coef[2, i]
                exponent = (px * px + py * py + pz * pz) * coef[3, i]
                skew = (px * coef[5, i] + py * coef[6, i] + pz * coef[7, i]) * (exponent + 2.5)
                weight = jnp.exp(exponent)
                power[b, s] = exponent
                bell[b, s] = weight
                target = coef[4, i] * weight * (1.0 + skew)
                source = jnp.where(cells[1, i] > 0.5, wall, target)
                one = att[b, s]
                running = one * running + (1.0 - one) * source
                gain[b, s] = running
            message[k - 1, q * rows : (q + 1) * rows] = running
        message[k - 1, own * rows : own * rows + 1] = depth_row

        @pl.when(k < group_size)
        def _():
            send_to(k, message.at[k - 1], arrived, out_send, out_recv, in_group)

        return carry

    lax.fori_loop(1, group_size + 1, sweep, 0)
    arrived[group_size - 1] = message[group_size - 1]

    def gain_sums(b, sums):
        backward = lax.rem(octant_ref[b], 2)
        weight, weight_e = table[WEIGHT, b], table[WEIGHT_E, b]
        sums = list(sums)
        for i in range(columns):
            value = gain[b, i + backward * (columns - 1 - 2 * i)]
            sums[i] = sums[i] + value * weight
            sums[columns + i] = sums[columns + i] + value * weight_e
        return tuple(sums)

    sums = lax.fori_loop(0, blocks, gain_sums, (zero_tile,) * (2 * columns))
    for n in range(2 * columns):
        half_sums[n] = sums[n]

    out_copies = all_copies(group_size - 1, arrived, out_send, out_recv, in_group)
    out_copies.wait_recv()

    group_depth = zero_tile
    for j in range(group_size):
        row = jnp.broadcast_to(arrived[j, own * rows : own * rows + 1], (rows, LANES))
        depth = jnp.sum(jnp.where(diagonal, row, 0.0), axis=1, keepdims=True)
        depths[j] = jnp.broadcast_to(depth, (rows, LANES))
        group_depth = group_depth + depths[j]
    backwards = [lax.rem(octant_ref[own * pos + q], 2) for q in range(own)]
    for q in range(own):
        neg_inv = table[NEG_INV, own * pos + q]
        kept, running = jnp.ones((rows, LANES), F32), zero_tile
        for s in range(group_size):
            t = slot_of(s + backwards[q] * (group_size - 1 - 2 * s), pos, group_size)
            prefix[0, q, s] = kept
            prefix[1, q, s] = running
            one = jnp.exp(depths[t] * neg_inv)
            running = one * running + arrived[t, q * rows : (q + 1) * rows]
            kept = kept * one
        joint[q] = running
    joint[own] = group_depth

    for k in range(1, groups):
        send_to(k, joint, joint_slots, joint_send, joint_recv, in_joint)
    joint_slots[groups - 1] = joint[...]
    joint_copies = all_copies(groups - 1, joint_slots, joint_send, joint_recv, in_joint)
    joint_copies.wait_recv()
    entering = []
    for q in range(own):
        neg_inv = table[NEG_INV, own * pos + q]
        state = inflow_ref[backwards[q], :, q * LANES : (q + 1) * LANES]
        place = group + backwards[q] * (groups - 1 - 2 * group)
        for s in range(groups - 1):
            g = slot_of(s + backwards[q] * (groups - 1 - 2 * s), group, groups)
            before = jnp.broadcast_to((place - s).astype(F32), (rows, LANES)) > 0.5
            longer = jnp.exp(joint_slots[g, own] * neg_inv) * state + joint_slots[g, q]
            state = jnp.where(before, longer, state)
        entering.append(state)

    for k in range(1, group_size + 1):
        j = lax.rem(pos + k, group_size)
        for q in range(own):
            s = j + backwards[q] * (group_size - 1 - 2 * j)
            result[k - 1, q] = prefix[0, q, s] * entering[q] + prefix[1, q, s]
        if k < group_size:
            send_to(k, result.at[k - 1], incoming, back_send, back_recv, in_group)
    incoming[group_size - 1] = result[group_size - 1]
    back_copies = all_copies(group_size - 1, incoming, back_send, back_recv, in_group)
    back_copies.wait_recv()

    def entering_tile(b):
        return incoming[slot_of(lax.div(b, own), pos, group_size), lax.rem(b, own)]

    def halves(b, sums):
        sums = list(sums)
        backward = lax.rem(octant_ref[b], 2)
        weight, weight_e = table[WEIGHT, b], table[WEIGHT_E, b]
        enter = entering_tile(b)
        for i in range(columns):
            value = decay[b, i + backward * (columns - 1 - 2 * i)] * enter
            sums[i] = sums[i] + value * weight
            sums[columns + i] = sums[columns + i] + value * weight_e
        return tuple(sums)

    sums = tuple(half_sums[n] for n in range(2 * columns))
    sums = lax.fori_loop(0, blocks, halves, sums)
    packed = extra[0]
    for n in range(2 * columns):
        packed = jnp.where(lane == n, jnp.sum(sums[n], axis=1, keepdims=True), packed)
    tile[...] = packed

    for k in range(1, count):
        send_to(k, tile, tile_slots, tile_send, tile_recv, in_vert)
    for n, (side, k) in enumerate(lines):
        pltpu.make_async_remote_copy(
            src_ref=tile, dst_ref=line_slots.at[n], send_sem=line_send, recv_sem=line_recv,
            device_id=in_line(side, k), device_id_type=MESH,
        ).start()

    def form(b, carry):
        backward = lax.rem(octant_ref[b], 2)
        enter = entering_tile(b)
        for i in range(columns):
            s = i + backward * (columns - 1 - 2 * i)
            out_ref[i, :, lane_block(b)] = decay[b, s] * enter + gain[b, s]
        return carry

    lax.fori_loop(0, blocks, form, 0)

    tile_copies = all_copies(count - 1, tile_slots, tile_send, tile_recv, in_vert)
    tile_copies.wait_recv()
    total = tile[...]
    for k in range(count - 1):
        total = total + tile_slots[k]
    tiles_ref[1] = jnp.where(lane < 2 * columns, total, packed)

    def one_line(value):
        return in_line(0, value)

    line_copies = all_copies(len(lines), line_slots, line_send, line_recv, one_line)
    line_copies.wait_recv()
    for side, edge in ((0, 0), (2, wide - 1)):
        slots = [line_slots[n] for n, (other, _) in enumerate(lines) if other == side]
        total = slots[0]
        for slot in slots[1:]:
            total = total + slot
        total = jnp.where(lane < 2 * columns, total, slots[0])
        tiles_ref[side] = jnp.where(col == edge, 0.0, total)
    for copies in (
        vert_copies, out_copies, joint_copies, back_copies, tile_copies, line_copies
    ):
        copies.wait_send()

    rho, warmth, flow_sq, scale = (extra[1 + n] for n in range(4))
    change_rho, change_energy = corrections(tiles_ref)
    change_warmth = (2.0 * change_energy / 3.0 - (warmth + flow_sq / 3.0) * change_rho) / rho
    ratio_rho = change_rho / rho
    ratio_warmth = change_warmth / warmth
    level, slope = scale * (ratio_rho - 1.5 * ratio_warmth), -(scale * ratio_warmth)

    def finish_columns(low, high):
        levels = [spread(level, i, rows) for i in range(low, high)]
        slopes = [spread(slope, i, rows) for i in range(low, high)]

        def finish(b, carry):
            backward = lax.rem(octant_ref[b], 2)
            for n, i in enumerate(range(low, high)):
                s = i + backward * (columns - 1 - 2 * i)
                change = bell[b, s] * (levels[n] + slopes[n] * power[b, s])
                out_ref[i, :, lane_block(b)] = out_ref[i, :, lane_block(b)] + change
            return carry

        lax.fori_loop(0, blocks, finish, 0)

    finish_columns(0, columns // 2)
    finish_columns(columns // 2, columns)


def corrections(tiles_ref):
    rows = tiles_ref.shape[1]
    lane, row = lane_index(rows), row_index(rows)

    def joined(n):
        def moved(side, start, place):
            shift = (place - 16 * n - start) % LANES
            return pltpu.roll(tiles_ref[side], shift, 1) if shift else tiles_ref[side]

        value = jnp.where(lane < 4, moved(0, 12, 0), moved(1, 0, 4))
        value = jnp.where(lane < 20, value, moved(2, 0, 20))
        return jnp.where(lane < 24, value, 0.0)

    warmth = joined(2)
    residuals = [joined(0) - joined(3), joined(1) - joined(4)]
    edges = (row == 0).astype(F32) + (row == rows - 1).astype(F32)
    scale = 1.0 / (1.0 + (4.0 - edges) * warmth)
    out = []
    for residual in residuals:
        value = residual * scale
        for _ in range(JAC):
            around = pltpu.roll(value, 1, 1) + pltpu.roll(value, LANES - 1, 1)
            around = around + jnp.where(row == 0, 0.0, pltpu.roll(value, 1, 0))
            around = around + jnp.where(row == rows - 1, 0.0, pltpu.roll(value, rows - 1, 0))
            value = (residual + warmth * around) * scale
        out.append(pltpu.roll(value, LANES - 4, 1))
    return out


def per_device(
    wide, count,
    prior_population, speeds, jacobian, octant, collision, solid_mask, wall_state, inflow,
):
    columns, rows, width = prior_population.shape
    blocks = width // LANES
    group_size = min(wide, blocks // 2)
    own = blocks // group_size
    groups = wide // group_size
    assert groups * group_size == wide and own * group_size == blocks and columns == 16
    shape = jax.ShapeDtypeStruct
    stays = pl.BlockSpec(memory_space=pltpu.HBM)

    def tiles(*lead):
        return pltpu.VMEM(lead + (rows, LANES), F32)

    def dma(*counts):
        return pltpu.SemaphoreType.DMA(counts)

    arguments = [
        pltpu.with_memory_space_constraint(value, pltpu.HBM)
        for value in (
            octant, speeds, jacobian.reshape(1, width), wall_state.reshape(1, width),
            collision.T, solid_mask.T, inflow, prior_population,
        )
    ]
    return pl.pallas_call(
        functools.partial(fused_kernel, wide, count, group_size),
        out_shape=shape((columns, rows, width), F32),
        in_specs=[stays] * 8,
        out_specs=pl.BlockSpec(memory_space=pltpu.VMEM),
        scratch_shapes=[
            pltpu.SMEM((blocks,), jnp.int32),
            pltpu.VMEM((3, width), F32),
            pltpu.VMEM((1, width), F32),
            pltpu.VMEM((1, width), F32),
            pltpu.VMEM((rows, columns), F32),
            pltpu.VMEM((rows, columns), jnp.int32),
            pltpu.VMEM((2, rows, own * LANES), F32),
            pltpu.VMEM((columns, rows, width), F32),
            tiles(7, blocks),
            pltpu.VMEM((16, width), F32),
            tiles(2, columns),
            tiles(blocks, columns),
            tiles(blocks, columns),
            tiles(blocks, columns),
            tiles(blocks, columns),
            tiles(blocks, columns),
            tiles(8, columns),
            tiles(5),
            tiles(2 * columns),
            tiles(3),
            pltpu.VMEM((rows, 2 * LANES), F32),
            pltpu.VMEM((count, rows, 2 * LANES), F32),
            pltpu.VMEM((group_size, own * rows + 1, LANES), F32),
            pltpu.VMEM((group_size, own * rows + 1, LANES), F32),
            tiles(group_size),
            tiles(2, own, group_size),
            tiles(own + 1),
            tiles(groups, own + 1),
            tiles(group_size, own),
            tiles(group_size, own),
            tiles(),
            tiles(count),
            tiles(2 * count),
            dma(7), dma(CHUNKS),
        ] + [pltpu.SemaphoreType.DMA] * 12 + [
        ],
        compiler_params=pltpu.CompilerParams(
            collective_id=0, has_side_effects=True, vmem_limit_bytes=40 * 1024 * 1024
        ),
    )(*arguments)


def solution(mesh):
    in_specs = (
        P("gx", None, "vert"),
        P(None, "vert"),
        P("vert"),
        P("vert"),
        P("gx", None),
        P("gx", None),
        P("vert"),
        P(None, None, "vert"),
    )
    return jax.shard_map(
        functools.partial(per_device, mesh.shape["gx"], mesh.shape["vert"]),
        mesh=mesh,
        in_specs=in_specs,
        out_specs=P("gx", None, "vert"),
        check_vma=False,
    )
```
